128 devices in a mesh: table: 16 (over y, x), col: 8 (over z, core).
Axes of the slice: x: 4, y: 4, z: 4, core: 2. Of those that a mesh axis runs over, the one named last changes fastest.
Arguments:
- table_rows: float32 [32768, 512], P('table', 'col'), may hold values from -6 to 6
- ada_state: float32 [32768], P('table'), may hold values from 0.5 to 20
- w_uvqk: bfloat16 [512, 2048], replicated, may hold values from -0.25 to 0.25
- w_out: bfloat16 [512, 512], replicated, may hold values from -0.25 to 0.25
- tok_owner: int32 [16, 5120, 1], P('table'), may hold values from 0 to 15; in each aligned block of 640 rows (0 to 639, 640 to 1279, ..., all dimensions but the last counted through in order) at most 80 rows name the same one
- tok_slot: int32 [16, 5120], P('table'), may hold values from 0 to 2047
- seg_ids: int32 [128, 640], P(('table', 'col')), may hold values from 0 to 7, never falling along the last dimension, each value on 1 to 160 neighbouring positions
- cotangent: bfloat16 [81920, 512], P(('table', 'col')), may hold values from -60 to 60
Outputs:
- layer_out: bfloat16 [81920, 512], P(('table', 'col'))
- new_table: float32 [32768, 512], P('table', 'col')
- new_state: float32 [32768], P('table')
The draws below stay inside these ranges and needn't reach their ends.
Inputs may be any that keep to these rules, and one draw needn't show every extreme that they name: `tok_owner`: among the 640 tokens of one device, at most 80 name any one table index. `seg_ids`: along each device's row the sequence numbers never fall; a sequence holds at most 160 tokens.
All inputs are finite; a program needn't handle non-finite values.
Results may differ from the reference program's by a relative error of at most 0.0066.
Values may be sent and summed in bfloat16 or wider, within the bound.
No kernel may reach another device: no remote copies, remote signals or barrier semaphores. Data moves between devices by JAX's collectives and lax.ppermute only.
A program may use at most 128 MiB of HBM per device.

```python
import math
import jax
import jax.numpy as jnp
import numpy as np
from jax import lax

D = 512
HEADS = 4
HDIM = 128
TOK_DEV = 640
TOUCH_DEV = 2048
SEQ_DEV = 8
MAXLEN = 160
CAP = 80
GROUP = 5120
TOKENS = 81920
TOUCHED = 32768
N_TABLE = 16
DEVICES = 128


def draw_cotangent(key, part):
    key = jax.random.fold_in(key, 7)
    first, second, third = jax.random.split(key, 3)
    column = jnp.arange(D, dtype=jnp.float32) / D
    column_scale = 10.0 ** column * jax.random.uniform(second, (D,), jnp.float32, 0.5, 2.0)
    base = jnp.clip(jax.random.normal(first, (TOKENS, D), jnp.float32), -6.0, 6.0)
    row_scale = jax.random.uniform(third, (TOKENS, 1), jnp.float32, 0.5, 2.0)
    return (0.25 * base * column_scale[None, :] * row_scale).astype(jnp.bfloat16)


def plant(values, rng, smallest, largest):
    extent = values.shape
    place = [jax.random.randint(jax.random.fold_in(rng, axis), (), 0, extent[axis]) for axis in range(len(extent))]
    values = values.at[tuple(place)].set(smallest)
    longest = extent.index(max(extent))
    place[longest] = (place[longest] + 1) % extent[longest]
    return values.at[tuple(place)].set(largest)


def shard_levels(rng, shape, cuts, low, largest):
    def one(position, parts):
        steps = jax.random.uniform(jax.random.fold_in(jax.random.fold_in(rng, 6), position), (parts,), jnp.float32, low / len(cuts), largest / len(cuts))
        return jnp.repeat(jnp.exp(steps), shape[position] // parts).reshape((-1,) + (1,) * (len(shape) - position - 1))

    factor_of = one(*cuts[0])
    for cut in cuts[1:]:
        factor_of = factor_of * one(*cut)
    return factor_of


def profile(number_of, total, bound, lean):
    loads = [(1 << 20) // math.isqrt(rank ** lean) + 1 for rank in range(2, number_of + 1)]
    rest, counts = total - bound - (number_of - 1), [1] * (number_of - 1)
    while rest > 0:
        movable = [i for i in range(number_of - 1) if counts[i] < bound]
        whole, remaining = sum([loads[i] for i in movable]), rest
        for i in movable:
            extra = min(bound - counts[i], max(1, remaining * loads[i] // whole), rest)
            counts[i] = counts[i] + extra
            rest = rest - extra
    return np.array([bound] + counts)


def uneven_parts(key, count, total, limit, slope):
    if count == 2:
        one = jax.random.randint(key, (), max(1, total - limit), min(limit, total - 1) + 1)
        return jnp.stack([one, total - one])
    sizes = jnp.asarray(profile(count, total, limit, slope), jnp.int32)
    couples = (count - 1) // 2
    donor, taker = sizes[1:1 + 2 * couples:2], sizes[2:2 + 2 * couples:2]
    room = jnp.minimum(donor - 1, limit - taker)
    moved = jax.random.randint(jax.random.fold_in(key, 1), (couples,), 0, 1 << 20) % (room + 1)
    sizes = sizes.at[1:1 + 2 * couples:2].set(donor - moved).at[2:2 + 2 * couples:2].set(taker + moved)
    return sizes[jax.random.permutation(jax.random.fold_in(key, 2), count)]


def routed_block(stream_key, own, number, rows, count, top, most, skew):
    order = jax.random.permutation(stream_key, count)
    packed, common = portions_of(count, rows * top, most, skew, True), portions_of(count, rows * top, most, skew, False)
    places = jnp.arange(count)

    def named(tallies, turn):
        used = int((tallies > 0).sum())
        fixed = max(1, used // 4)
        shifted = fixed + (places - fixed + turn * (used - fixed)) % max(1, count - fixed)
        return jnp.zeros((count,), jnp.int32).at[order[jnp.where(places < fixed, places, shifted)]].set(jnp.asarray(tallies, jnp.int32))

    tallies = jnp.where(number % 4 == 0, named(packed, number // 4), named(common, number - number // 4 - 1))
    mixed = jax.random.permutation(jax.random.fold_in(own, 3), count)
    giver, taker = mixed[0:count // 2 * 2:2], mixed[1:count // 2 * 2:2]
    margin = jnp.minimum(tallies[giver] - 1, most - tallies[taker]) // 2
    margin = jnp.where((giver == order[0]) | (taker == order[0]) | (tallies[taker] == 0), 0, jnp.maximum(margin, 0))
    shifted = jax.random.randint(jax.random.fold_in(own, 4), (count // 2,), 0, 1 << 20) % (margin + 1)
    tallies = tallies.at[giver].add(-shifted).at[taker].add(shifted)
    labels = jnp.searchsorted(jnp.cumsum(tallies), jnp.arange(rows * top), side="right").astype(jnp.int32)
    listing = labels.reshape(top, rows).T
    listing = listing[jax.random.permutation(jax.random.fold_in(own, 1), rows)]
    turn = jax.random.randint(jax.random.fold_in(own, 2), (rows, 1), 0, top)
    return jnp.take_along_axis(listing, (jnp.arange(top)[None, :] + turn) % top, axis=1)


def portions_of(number_of, total, most, slope, full):
    weights = [(1 << 20) // math.isqrt(standing ** slope) + 1 for standing in range(1, number_of + 1)]
    largest = most if full else min(most, max(-(-total // number_of), total * weights[0] // sum(weights)))
    least = 1 if total - largest >= number_of - 1 else 0
    holding, surplus = [largest] + [least] * (number_of - 1), total - largest - least * (number_of - 1)
    while surplus > 0:
        movable = [i for i in range(1, number_of) if holding[i] < largest] or [i for i in range(1, number_of) if holding[i] < most]
        mass, left = sum([weights[i] for i in movable]), surplus
        for i in movable:
            addition = min(most - holding[i], max(1, left * weights[i] // mass), surplus)
            holding[i] = holding[i] + addition
            surplus = surplus - addition
    return np.array(holding)


def normal_values(stream_key, extent, scale, most, cuts=(), kind=jnp.bfloat16):
    values = scale * jax.random.normal(stream_key, extent, jnp.float32)
    if cuts:
        values = values * shard_levels(stream_key, extent, cuts, -0.22, 0.18)
    return jnp.clip(values, -most, most).astype(kind)


def setup_inputs(seed: int = 0) -> dict:
    splits = jax.random.split(jax.random.key(seed), 9)
    table_rows = normal_values(splits[0], (TOUCHED, D), 1.0, 6.0, ((0, 16), (1, 8)), jnp.float32)
    ada_state = jnp.clip(jnp.exp(math.log(20.0) - 3.6888795 * jax.random.uniform(splits[1], (TOUCHED,), jnp.float32) ** shard_levels(splits[1], (TOUCHED,), ((0, 16),), -0.2, 0.2)), 0.5, 20.0)
    w_uvqk = normal_values(splits[2], (D, 4 * HEADS * HDIM), D ** -0.5, 0.25)
    w_out = normal_values(splits[3], (HEADS * HDIM, D), (HEADS * HDIM) ** -0.5, 0.25)
    tok_owner_keys = jax.random.split(jax.random.fold_in(splits[4], 1), N_TABLE * GROUP // TOK_DEV)
    tok_owner_turns = jax.random.permutation(jax.random.fold_in(splits[4], 3), N_TABLE * GROUP // TOK_DEV)
    tok_owner = jax.vmap(lambda own, number: routed_block(jax.random.fold_in(splits[4], 2), own, number, TOK_DEV, N_TABLE, 1, CAP, 2))(tok_owner_keys, tok_owner_turns).reshape((N_TABLE, GROUP, 1))
    tok_slot = plant(jax.random.randint(splits[5], (N_TABLE, GROUP), 0, TOUCH_DEV), jax.random.fold_in(splits[5], 1), 0, TOUCH_DEV - 1).astype(jnp.int32)
    seg_ids = jax.vmap(lambda own: jnp.searchsorted(jnp.cumsum(uneven_parts(own, SEQ_DEV, TOK_DEV, MAXLEN, 2)), jnp.arange(TOK_DEV), side="right"))(jax.random.split(splits[6], DEVICES)).reshape((DEVICES, TOK_DEV)).astype(jnp.int32)
    cotangent = draw_cotangent(jax.random.fold_in(splits[8], 71), 0)
    return {"table_rows": table_rows, "ada_state": ada_state, "w_uvqk": w_uvqk, "w_out": w_out, "tok_owner": tok_owner, "tok_slot": tok_slot, "seg_ids": seg_ids, "cotangent": cotangent}


NORM_EPS = 1e-05
ROOT_EPS = 1e-08
STEP_SIZE = 0.3

def layer_norm(values):
    center = values - lax.optimization_barrier(jnp.mean(values, axis=-1, keepdims=True))
    spread = lax.optimization_barrier(jnp.mean(center * center, axis=-1, keepdims=True))
    return center * lax.rsqrt(spread + NORM_EPS)

def hstu_layer(embedded, segment, w_uvqk, w_out):
    length = embedded.shape[0]
    width = HEADS * HDIM
    resid = embedded.astype(jnp.float32)
    normed = layer_norm(resid).astype(jnp.bfloat16)
    projected = jax.nn.silu(jnp.dot(normed, w_uvqk, preferred_element_type=jnp.float32))
    gates = projected[:, :width]
    values = projected[:, width:2 * width].astype(jnp.bfloat16).reshape(length, HEADS, HDIM)
    queries = projected[:, 2 * width:3 * width].astype(jnp.bfloat16).reshape(length, HEADS, HDIM)
    keyset = projected[:, 3 * width:].astype(jnp.bfloat16).reshape(length, HEADS, HDIM)
    scores = jnp.einsum('thd,shd->hts', queries.astype(jnp.float32), keyset.astype(jnp.float32))
    places = jnp.arange(length)
    allowed = (segment[:, None] == segment[None, :]) & (places[:, None] >= places[None, :])
    weights = jnp.where(allowed[None], jax.nn.silu(scores * HDIM ** (-0.5)), 0.0).astype(jnp.bfloat16)
    attended = jnp.einsum('hts,shd->thd', weights.astype(jnp.float32), values.astype(jnp.float32))
    gated = (layer_norm(attended.reshape(length, width)) * gates).astype(jnp.bfloat16)
    return jnp.dot(gated, w_out, preferred_element_type=jnp.float32) + resid

def reference(table_rows, ada_state, w_uvqk, w_out, tok_owner, tok_slot, seg_ids, cotangent):
    table_bf = table_rows.astype(jnp.bfloat16)
    index = (tok_owner[..., 0] * TOUCH_DEV + tok_slot).astype(jnp.int32).reshape(DEVICES, TOK_DEV)
    tangents = cotangent.reshape(DEVICES, TOK_DEV, D)

    def one_device(operands):
        row_index, segment, tangent = operands
        embedded = jnp.take(table_bf, row_index, axis=0)
        result, pullback = jax.vjp(lambda rows_in: hstu_layer(rows_in, segment, w_uvqk, w_out), embedded)
        token_grad, = pullback(tangent.astype(result.dtype))
        return (result.astype(jnp.bfloat16), token_grad)
    outputs, grads = lax.map(one_device, (index, seg_ids, tangents))
    row_grad = jnp.zeros((TOUCHED, D), jnp.float32).at[index.reshape(-1)].add(grads.reshape(-1, D).astype(jnp.float32))
    new_state = ada_state + lax.optimization_barrier(jnp.sum(row_grad * row_grad, axis=1)) / D
    new_table = table_rows - STEP_SIZE * row_grad / (jnp.sqrt(new_state)[:, None] + ROOT_EPS)
    return (outputs.reshape(TOKENS, D), new_table, new_state)
```

```python
import functools

import jax
import jax.numpy as jnp
from jax import lax
from jax.experimental import pallas as pl
from jax.experimental.pallas import tpu as pltpu
from jax.sharding import PartitionSpec as P

D = 512
HEADS = 4
HDIM = 128
TOK_DEV = 640
TABLES = 16
COLS = 8
CAP = 80
HALF = CAP // 2
TOUCH = 2048
WIDTH = D // COLS
HI = 256
HI_BITS = 8
LO = TOUCH // HI
ASKS = 768
BLOCK = 128
MAXLEN = 160

NORM_EPS = 1e-05
ROOT_EPS = 1e-08
STEP_SIZE = 0.3

F32 = jnp.float32
BF16 = jnp.bfloat16
I32 = jnp.int32
VMEM_BYTES = 48 * 1024 * 1024


def iota(shape, dim):
    return lax.broadcasted_iota(I32, shape, dim)


def nt_dot(a, b):
    return lax.dot_general(a, b, (((1,), (1,)), ((), ())), preferred_element_type=F32)


def tn_dot(a, b):
    return lax.dot_general(a, b, (((0,), (0,)), ((), ())), preferred_element_type=F32)


def params():
    return pltpu.CompilerParams(vmem_limit_bytes=VMEM_BYTES)


def ask_kernel(owner_ref, slot_ref, asks_ref, place_ref):
    lower = jnp.where(iota((TOK_DEV, TOK_DEV), 0) <= iota((TOK_DEV, TOK_DEV), 1), 1.0, 0.0).astype(BF16)
    table = iota((TABLES, TOK_DEV), 0)
    spans = [slice(TOK_DEV * m, TOK_DEV * (m + 1)) for m in range(COLS)]
    hits = [jnp.where(owner_ref[:, span] == table, 1.0, 0.0) for span in spans]
    running = jnp.dot(
        jnp.concatenate(hits, axis=0).astype(BF16), lower, preferred_element_type=F32
    )
    lane = iota((TABLES, 128), 1)
    slot_at = iota((128, TOK_DEV), 0)
    tiles = [jnp.zeros((TABLES, 128), F32) for _ in range(ASKS // 128)]
    for m, span in enumerate(spans):
        count = running[TABLES * m : TABLES * (m + 1)] * hits[m]
        placing = jnp.sum(count, axis=0, keepdims=True).astype(I32) - 1
        onehot = jnp.where(slot_at == placing, 1.0, 0.0).astype(BF16)
        slot = slot_ref[:, span]
        high = (slot >> HI_BITS).astype(F32) * hits[m]
        low = (slot & (HI - 1)).astype(F32) * hits[m]
        found = nt_dot(jnp.concatenate([high, low], axis=0).astype(BF16), onehot)
        value = found[:TABLES] * float(HI) + found[TABLES:]
        for h in range(2):
            begin = h * (ASKS // 2) + m * HALF
            moved = pltpu.roll(value, (begin - h * HALF) % 128, 1)
            for j in range(begin // 128, (begin + HALF - 1) // 128 + 1):
                at = lane + 128 * j
                tiles[j] = jnp.where((at >= begin) & (at < begin + HALF), moved, tiles[j])
        place_ref[m : m + 1, :] = (
            owner_ref[:, span] * HALF
            + placing
            + jnp.where(placing >= HALF, TABLES * HALF - HALF, 0)
        )
    for j, tile in enumerate(tiles):
        asks_ref[:, 0, 128 * j : 128 * (j + 1)] = tile.astype(I32)


def make_asks(owner, slot):
    return pl.pallas_call(
        ask_kernel,
        out_shape=(
            jax.ShapeDtypeStruct((TABLES, 1, ASKS), I32),
            jax.ShapeDtypeStruct((COLS, TOK_DEV), I32),
        ),
        compiler_params=params(),
        name="ask",
    )(owner, slot)


def ask_onehot(ask):
    return jnp.where(iota((HI, ASKS), 0) == (ask & (HI - 1)), 1.0, 0.0).astype(BF16)


def pick_kernel(parity, asks_ref, table_ref, reply_ref, rows_ref):
    par = parity()
    for lo in range(LO):
        rows_ref[WIDTH * lo : WIDTH * (lo + 1), :] = table_ref[:, HI * lo : HI * (lo + 1)].astype(BF16)

    def one_group(g, carry):
        ask = asks_ref[g]
        found = jnp.dot(rows_ref[...], ask_onehot(ask), preferred_element_type=F32)
        low = jnp.broadcast_to(ask >> HI_BITS, (WIDTH, ASKS))
        kept = found[:WIDTH]
        for lo in range(1, LO):
            kept = jnp.where(low == lo, found[WIDTH * lo : WIDTH * (lo + 1)], kept)
        first, second = kept[:, : ASKS // 2], kept[:, ASKS // 2 :]
        stacked = jnp.concatenate(
            [jnp.where(par == 0, first, second), jnp.where(par == 0, second, first)], axis=0
        )
        reply_ref[g] = stacked.T[: COLS * HALF].astype(BF16)
        return carry

    lax.fori_loop(0, TABLES, one_group, 0)


def pick_rows(asks, table_t, parity):
    return pl.pallas_call(
        functools.partial(pick_kernel, parity),
        out_shape=jax.ShapeDtypeStruct((TABLES, COLS * HALF, 128), BF16),
        scratch_shapes=[pltpu.VMEM((LO * WIDTH, HI), BF16)],
        compiler_params=params(),
        name="pick",
    )(asks, table_t)


def add_kernel(parity, asks_ref, arrived_ref, grad_ref, squares_ref, total_ref):
    par = parity()
    total_ref[...] = jnp.zeros_like(total_ref)
    empty = jnp.zeros((ASKS // 2 - COLS * HALF, 128), F32)

    def one_group(g, carry):
        ask = asks_ref[g]
        block = jnp.concatenate([arrived_ref[g].astype(F32), empty], axis=0).T
        upper, lower = block[:WIDTH], block[WIDTH:]
        slots = jnp.concatenate(
            [jnp.where(par == 0, upper, lower), jnp.where(par == 0, lower, upper)], axis=1
        )
        low = jnp.broadcast_to(ask >> HI_BITS, (WIDTH, ASKS))
        spread = jnp.concatenate(
            [jnp.where(low == lo, slots, 0.0).astype(BF16) for lo in range(LO)], axis=0
        )
        total_ref[...] += nt_dot(spread, ask_onehot(ask))
        return carry

    lax.fori_loop(0, TABLES, one_group, 0)
    sums = []
    for lo in range(LO):
        part = total_ref[WIDTH * lo : WIDTH * (lo + 1), :]
        grad_ref[:, HI * lo : HI * (lo + 1)] = part
        square = jnp.sum(part * part, axis=0, keepdims=True)
        sums += [square[:, :128], square[:, 128:]]
    squares = jnp.concatenate(sums, axis=0)
    for c in range(COLS):
        squares_ref[c] = squares


def add_rows(asks, arrived, parity):
    return pl.pallas_call(
        functools.partial(add_kernel, parity),
        out_shape=(
            jax.ShapeDtypeStruct((WIDTH, TOUCH), F32),
            jax.ShapeDtypeStruct((COLS, TOUCH // 128, 128), F32),
        ),
        scratch_shapes=[pltpu.VMEM((LO * WIDTH, HI), F32)],
        compiler_params=params(),
        name="add",
    )(asks, arrived)


def update_kernel(squares_ref, state_ref, table_ref, grad_ref, new_table_ref, new_state_ref):
    squares = squares_ref[0]
    for c in range(1, COLS):
        squares = squares + squares_ref[c]
    state = state_ref[...] + squares / D
    new_state_ref[...] = state
    factor = STEP_SIZE / (jnp.sqrt(state) + ROOT_EPS)
    for i in range(TOUCH // 128):
        at = slice(128 * i, 128 * (i + 1))
        new_table_ref[:, at] = table_ref[:, at] - grad_ref[:, at] * factor[i : i + 1]


def update(squares, state, table_t, grad_t):
    return pl.pallas_call(
        update_kernel,
        out_shape=(
            jax.ShapeDtypeStruct((WIDTH, TOUCH), F32),
            jax.ShapeDtypeStruct((TOUCH // 128, 128), F32),
        ),
        compiler_params=params(),
        name="update",
    )(squares, state, table_t, grad_t)


def normalise(values):
    center = values - jnp.mean(values, axis=-1, keepdims=True)
    root = lax.rsqrt(jnp.mean(center * center, axis=-1, keepdims=True) + NORM_EPS)
    return center * root, root


def normalise_back(grad, normed, root):
    along = jnp.mean(grad * normed, axis=-1, keepdims=True)
    return root * (grad - jnp.mean(grad, axis=-1, keepdims=True) - normed * along)


def columns_of(row):
    return jnp.broadcast_to(row.astype(F32), (128, TOK_DEV)).T


def layer_kernel(
    member,
    received_ref,
    place_ref,
    segment_ref,
    w_ref,
    w_out_ref,
    cotangent_ref,
    out_ref,
    pieces_ref,
    slots_ref,
    place_col,
    segment_col,
    embedded_ref,
    normed_ref,
    root_ref,
    gates_ref,
    slope_ref,
    values_ref,
    queries_ref,
    keys_ref,
    grad_u_ref,
    grad_values_ref,
    grad_keys_ref,
    token_grad_ref,
):
    place = place_ref[pl.ds(member(), 1), :]
    place_col[...] = columns_of(place)
    segment_col[...] = columns_of(segment_ref[...])
    left = iota((HALF, 128), 1) < WIDTH
    blocks = TOK_DEV // BLOCK
    four = 4 * HALF

    def gather_slots(t, carry):
        parts = []
        for i in range(4):
            block = received_ref[4 * t + i].astype(F32)
            parts.append([block[HALF * c : HALF * (c + 1)] for c in range(COLS)])
        at = pl.multiple_of(four * t, four)
        for j in range(COLS // 2):
            pairs = [(part[2 * j], part[2 * j + 1]) for part in parts]
            first = [jnp.where(left, even, odd) for even, odd in pairs]
            second = [pltpu.roll(jnp.where(left, odd, even), WIDTH, 1) for even, odd in pairs]
            tile = slice(128 * j, 128 * (j + 1))
            slots_ref[pl.ds(at, four), tile] = jnp.concatenate(first, axis=0).astype(BF16)
            slots_ref[pl.ds(TABLES * HALF + at, four), tile] = jnp.concatenate(second, axis=0).astype(BF16)
        return carry

    lax.fori_loop(0, TABLES // 4, gather_slots, 0)

    def project(b, carry):
        rows = pl.ds(pl.multiple_of(BLOCK * b, BLOCK), BLOCK)
        at = place_col[rows, :].astype(I32)
        lane = iota((BLOCK, 128), 1)
        onehot = jnp.concatenate(
            [jnp.where(at == lane + 128 * j, 1.0, 0.0).astype(BF16) for j in range(TABLES * CAP // 128)],
            axis=1,
        )
        embedded = jnp.dot(onehot, slots_ref[...], preferred_element_type=F32)
        embedded_ref[rows, :] = embedded
        normed, root = normalise(embedded)
        normed = normed.astype(BF16)
        normed_ref[rows, :] = normed
        root_ref[rows, :] = jnp.broadcast_to(root, (BLOCK, 128))
        for j, ref in enumerate((gates_ref, values_ref, queries_ref, keys_ref)):
            part = slice(D * j, D * (j + 1))
            linear = jnp.dot(normed, w_ref[:, part], preferred_element_type=F32)
            gate = 0.5 + 0.5 * jnp.tanh(0.5 * linear)
            swish = linear * gate
            ref[rows, :] = swish.astype(ref.dtype)
            slope_ref[rows, part] = gate + swish * (1.0 - gate)
        return carry

    lax.fori_loop(0, blocks, project, 0)

    grad_values_ref[...] = jnp.zeros_like(grad_values_ref)
    grad_keys_ref[...] = jnp.zeros_like(grad_keys_ref)
    scale = HDIM**-0.5
    for b in range(blocks):
        rows = slice(BLOCK * b, BLOCK * (b + 1))
        begin = max(0, (BLOCK * b - MAXLEN + 1) // BLOCK * BLOCK)
        width = BLOCK * (b + 1) - begin
        span = slice(begin, begin + width)
        segment = jnp.concatenate([segment_col[rows, :]] * (width // 128), axis=1)
        allowed = (segment == segment_ref[:, span].astype(F32)) & (
            iota((BLOCK, width), 0) + (BLOCK * b - begin) >= iota((BLOCK, width), 1)
        )
        saved = []
        attended = []
        for h in range(HEADS):
            head = slice(HDIM * h, HDIM * (h + 1))
            scores = scale * nt_dot(queries_ref[rows, head], keys_ref[span, head])
            gate = 0.5 + 0.5 * jnp.tanh(0.5 * scores)
            swish = scores * gate
            weights = jnp.where(allowed, swish, 0.0).astype(BF16)
            slope = jnp.where(allowed, scale * (gate + swish * (1.0 - gate)), 0.0)
            saved.append((weights, slope))
            attended.append(jnp.dot(weights, values_ref[span, head], preferred_element_type=F32))
        normed, root = normalise(jnp.concatenate(attended, axis=1))
        gates = gates_ref[rows, :]
        gated = (normed * gates).astype(BF16)
        out = jnp.dot(gated, w_out_ref[...], preferred_element_type=F32) + embedded_ref[rows, :]
        out_ref[rows, :] = out.astype(BF16)
        grad_gated = nt_dot(cotangent_ref[rows, :], w_out_ref[...]).astype(BF16).astype(F32)
        grad_u_ref[rows, :D] = (grad_gated * normed * slope_ref[rows, :D]).astype(BF16)
        grad_attended = normalise_back(grad_gated * gates, normed, root).astype(BF16)
        for h in range(HEADS):
            head = slice(HDIM * h, HDIM * (h + 1))
            weights, slope = saved[h]
            grad_weights = nt_dot(grad_attended[:, head], values_ref[span, head])
            grad_scores = (grad_weights * slope).astype(BF16)
            grad_queries = jnp.dot(grad_scores, keys_ref[span, head], preferred_element_type=F32)
            part = slice(2 * D + HDIM * h, 2 * D + HDIM * (h + 1))
            grad_u_ref[rows, part] = (grad_queries * slope_ref[rows, part]).astype(BF16)
            grad_values_ref[span, head] += tn_dot(weights, grad_attended[:, head])
            grad_keys_ref[span, head] += tn_dot(grad_scores, queries_ref[rows, head])

    def project_back(b, carry):
        rows = pl.ds(pl.multiple_of(BLOCK * b, BLOCK), BLOCK)
        grad_u_ref[rows, D : 2 * D] = (grad_values_ref[rows, :] * slope_ref[rows, D : 2 * D]).astype(BF16)
        grad_u_ref[rows, 3 * D :] = (grad_keys_ref[rows, :] * slope_ref[rows, 3 * D :]).astype(BF16)
        grad = nt_dot(grad_u_ref[rows, :], w_ref[...])
        grad = normalise_back(grad, normed_ref[rows, :].astype(F32), root_ref[rows, :1])
        token_grad_ref[rows, :] = (grad + cotangent_ref[rows, :].astype(F32)).astype(BF16)
        return carry

    lax.fori_loop(0, blocks, project_back, 0)

    def send_slots(t, carry):
        halves = []
        for h in range(2):
            onehot = jnp.where(
                place - (TABLES * HALF * h + four * t) == iota((four, TOK_DEV), 0), 1.0, 0.0
            ).astype(BF16)
            halves.append(jnp.dot(onehot, token_grad_ref[...], preferred_element_type=F32))
        for i in range(4):
            parts = []
            for j in range(COLS // 2):
                tile = (slice(HALF * i, HALF * (i + 1)), slice(128 * j, 128 * (j + 1)))
                first, second = halves[0][tile], pltpu.roll(halves[1][tile], WIDTH, 1)
                parts += [jnp.where(left, first, second), jnp.where(left, second, first)]
            pieces_ref[4 * t + i] = jnp.concatenate(parts, axis=0).astype(BF16)
        return carry

    lax.fori_loop(0, TABLES // 4, send_slots, 0)


def layer(received, place, member, segment, w_uvqk, w_out, cotangent):
    return pl.pallas_call(
        functools.partial(layer_kernel, member),
        out_shape=(
            jax.ShapeDtypeStruct((TOK_DEV, D), BF16),
            jax.ShapeDtypeStruct((TABLES, COLS * HALF, 128), BF16),
        ),
        scratch_shapes=[
            pltpu.VMEM((TABLES * CAP, D), BF16),
            pltpu.VMEM((TOK_DEV, 128), F32),
            pltpu.VMEM((TOK_DEV, 128), F32),
            pltpu.VMEM((TOK_DEV, D), F32),
            pltpu.VMEM((TOK_DEV, D), BF16),
            pltpu.VMEM((TOK_DEV, 128), F32),
            pltpu.VMEM((TOK_DEV, D), F32),
            pltpu.VMEM((TOK_DEV, 4 * D), F32),
            pltpu.VMEM((TOK_DEV, D), BF16),
            pltpu.VMEM((TOK_DEV, D), BF16),
            pltpu.VMEM((TOK_DEV, D), BF16),
            pltpu.VMEM((TOK_DEV, 4 * D), BF16),
            pltpu.VMEM((TOK_DEV, D), F32),
            pltpu.VMEM((TOK_DEV, D), F32),
            pltpu.VMEM((TOK_DEV, D), BF16),
        ],
        compiler_params=params(),
        name="layer",
    )(received, place, segment, w_uvqk, w_out, cotangent)


def exchange(blocks):
    blocks = blocks.reshape(TABLES * COLS, HALF, 128)
    blocks = lax.all_to_all(blocks, ("table", "col"), split_axis=0, concat_axis=0, tiled=True)
    return blocks.reshape(TABLES, COLS * HALF, 128)


def shards(table_rows, ada_state, w_uvqk, w_out, tok_owner, tok_slot, seg_ids, cotangent):
    def member():
        return lax.axis_index("col")

    def parity():
        return lax.axis_index("col") % 2

    table_t = table_rows.T
    asks, place = make_asks(tok_owner.reshape(1, COLS * TOK_DEV), tok_slot)
    asked = lax.all_to_all(asks, "table", split_axis=0, concat_axis=0, tiled=True)
    received = exchange(pick_rows(asked, table_t, parity))
    layer_out, pieces = layer(received, place, member, seg_ids, w_uvqk, w_out, cotangent)
    arrived = exchange(pieces)
    grad_t, squares = add_rows(asked, arrived, parity)
    squares = lax.all_to_all(squares, "col", split_axis=0, concat_axis=0, tiled=True)
    new_table_t, new_state = update(
        squares, ada_state.reshape(TOUCH // 128, 128), table_t, grad_t
    )
    return (layer_out, new_table_t.T, new_state.reshape(TOUCH))


def solution(mesh):
    in_specs = (
        P("table", "col"),
        P("table"),
        P(),
        P(),
        P("table", None, None),
        P("table", None),
        P(("table", "col"), None),
        P(("table", "col"), None),
    )
    out_specs = (P(("table", "col"), None), P("table", "col"), P("table"))
    return jax.shard_map(shards, mesh=mesh, in_specs=in_specs, out_specs=out_specs, check_vma=False)
```

```python
import functools

import jax
import jax.numpy as jnp
from jax import lax
from jax.experimental import pallas as pl
from jax.experimental.pallas import tpu as pltpu
from jax.sharding import PartitionSpec as P

D = 512
HEADS = 4
HDIM = 128
TOK_DEV = 640
TABLES = 16
COLS = 8
CAP = 80
HALF = CAP // 2
TOUCH = 2048
WIDTH = D // COLS
HI = 256
HI_BITS = 8
LO = TOUCH // HI
ASKS = 768
BLOCK = 128
REACH = 288
REACH_TILES = 384
FAR = -1.0e4

NORM_EPS = 1e-05
ROOT_EPS = 1e-08
STEP_SIZE = 0.3

F32 = jnp.float32
BF16 = jnp.bfloat16
I32 = jnp.int32


def iota(shape, dim):
    return lax.broadcasted_iota(I32, shape, dim)


def nt_dot(a, b):
    return lax.dot_general(a, b, (((1,), (1,)), ((), ())), preferred_element_type=F32)


def tn_dot(a, b):
    return lax.dot_general(a, b, (((0,), (0,)), ((), ())), preferred_element_type=F32)


def params(megabytes):
    return pltpu.CompilerParams(vmem_limit_bytes=megabytes * 1024 * 1024)


def ask_kernel(owner_ref, slot_ref, asks_ref, place_ref):
    lower = jnp.where(iota((TOK_DEV, TOK_DEV), 0) <= iota((TOK_DEV, TOK_DEV), 1), 1.0, 0.0).astype(BF16)
    table = iota((TABLES, TOK_DEV), 0)
    spans = [slice(TOK_DEV * m, TOK_DEV * (m + 1)) for m in range(COLS)]
    hits = [jnp.where(owner_ref[:, span] == table, 1.0, 0.0) for span in spans]
    running = jnp.dot(
        jnp.concatenate(hits, axis=0).astype(BF16), lower, preferred_element_type=F32
    )
    lane = iota((TABLES, 128), 1)
    slot_at = iota((128, TOK_DEV), 0)
    tiles = [jnp.zeros((TABLES, 128), F32) for _ in range(ASKS // 128)]
    for m, span in enumerate(spans):
        count = running[TABLES * m : TABLES * (m + 1)] * hits[m]
        placing = jnp.sum(count, axis=0, keepdims=True).astype(I32) - 1
        onehot = jnp.where(slot_at == placing, 1.0, 0.0).astype(BF16)
        slot = slot_ref[:, span]
        high = (slot >> HI_BITS).astype(F32) * hits[m]
        low = (slot & (HI - 1)).astype(F32) * hits[m]
        found = nt_dot(jnp.concatenate([high, low], axis=0).astype(BF16), onehot)
        value = found[:TABLES] * float(HI) + found[TABLES:]
        for h in range(2):
            begin = h * (ASKS // 2) + m * HALF
            moved = pltpu.roll(value, (begin - h * HALF) % 128, 1)
            for j in range(begin // 128, (begin + HALF - 1) // 128 + 1):
                at = lane + 128 * j
                tiles[j] = jnp.where((at >= begin) & (at < begin + HALF), moved, tiles[j])
        place_ref[m : m + 1, :] = (
            owner_ref[:, span] * HALF
            + placing
            + jnp.where(placing >= HALF, TABLES * HALF - HALF, 0)
        )
    for j, tile in enumerate(tiles):
        asks_ref[:, 0, 128 * j : 128 * (j + 1)] = tile.astype(I32)


def make_asks(owner, slot):
    return pl.pallas_call(
        ask_kernel,
        out_shape=(
            jax.ShapeDtypeStruct((TABLES, 1, ASKS), I32),
            jax.ShapeDtypeStruct((COLS, TOK_DEV), I32),
        ),
        compiler_params=params(32),
        name="ask",
    )(owner, slot)


def ask_onehot(ask):
    rows = iota((HI, ASKS), 0).astype(F32).astype(BF16)
    wanted = (ask & (HI - 1)).astype(F32).astype(BF16)
    return jnp.where(rows == wanted, jnp.ones((), BF16), jnp.zeros((), BF16))


def rows_kernel(table_ref, rows_ref):
    for lo in range(LO):
        rows_ref[WIDTH * lo : WIDTH * (lo + 1), :] = table_ref[:, HI * lo : HI * (lo + 1)].astype(BF16)


def make_rows(table_t):
    return pl.pallas_call(
        rows_kernel,
        out_shape=jax.ShapeDtypeStruct((LO * WIDTH, HI), BF16),
        compiler_params=params(8),
        name="rows",
    )(table_t)


def pick_kernel(parity, asks_ref, rows_ref, reply_ref):
    par = parity()

    def one_group(g, carry):
        ask = asks_ref[g]
        found = jnp.dot(rows_ref[...], ask_onehot(ask), preferred_element_type=F32)
        low = jnp.broadcast_to(ask >> HI_BITS, (WIDTH, ASKS))
        parts = [found[WIDTH * lo : WIDTH * (lo + 1)] for lo in range(LO)]
        for bit in (1, 2, 4):
            upper = (low & bit) != 0
            parts = [jnp.where(upper, parts[i + 1], parts[i]) for i in range(0, len(parts), 2)]
        kept = parts[0]
        first, second = kept[:, : ASKS // 2], kept[:, ASKS // 2 :]
        stacked = jnp.concatenate(
            [jnp.where(par == 0, first, second), jnp.where(par == 0, second, first)], axis=0
        )
        reply_ref[g] = stacked.T[: COLS * HALF].astype(BF16)
        return carry

    lax.fori_loop(0, TABLES, one_group, 0, unroll=8)


def pick_rows(asks, rows, parity):
    return pl.pallas_call(
        functools.partial(pick_kernel, parity),
        out_shape=jax.ShapeDtypeStruct((TABLES, COLS * HALF, 128), BF16),
        compiler_params=params(32),
        name="pick",
    )(asks, rows)


def add_kernel(parity, asks_ref, arrived_ref, grad_ref, squares_ref, total_ref):
    par = parity()
    total_ref[...] = jnp.zeros_like(total_ref)
    empty = jnp.zeros((ASKS // 2 - COLS * HALF, 128), F32)

    def one_group(g, carry):
        ask = asks_ref[g]
        block = jnp.concatenate([arrived_ref[g].astype(F32), empty], axis=0).T
        upper, lower = block[:WIDTH], block[WIDTH:]
        slots = jnp.concatenate(
            [jnp.where(par == 0, upper, lower), jnp.where(par == 0, lower, upper)], axis=1
        )
        low = jnp.broadcast_to(ask >> HI_BITS, (WIDTH, ASKS))
        spread = jnp.concatenate(
            [jnp.where(low == lo, slots, 0.0).astype(BF16) for lo in range(LO)], axis=0
        )
        total_ref[...] += nt_dot(spread, ask_onehot(ask))
        return carry

    lax.fori_loop(0, TABLES, one_group, 0, unroll=16)
    sums = []
    for lo in range(LO):
        part = total_ref[WIDTH * lo : WIDTH * (lo + 1), :]
        grad_ref[:, HI * lo : HI * (lo + 1)] = part
        square = jnp.sum(part * part, axis=0, keepdims=True)
        sums += [square[:, :128], square[:, 128:]]
    squares = jnp.concatenate(sums, axis=0)
    for c in range(COLS):
        squares_ref[c] = squares


def add_rows(asks, arrived, parity):
    return pl.pallas_call(
        functools.partial(add_kernel, parity),
        out_shape=(
            jax.ShapeDtypeStruct((WIDTH, TOUCH), F32),
            jax.ShapeDtypeStruct((COLS, TOUCH // 128, 128), F32),
        ),
        scratch_shapes=[pltpu.VMEM((LO * WIDTH, HI), F32)],
        compiler_params=params(48),
        name="add",
    )(asks, arrived)


def update_kernel(squares_ref, state_ref, table_ref, grad_ref, new_table_ref, new_state_ref):
    squares = squares_ref[0]
    for c in range(1, COLS):
        squares = squares + squares_ref[c]
    state = state_ref[...] + squares / D
    new_state_ref[...] = state
    factor = STEP_SIZE / (jnp.sqrt(state) + ROOT_EPS)
    for i in range(TOUCH // 128):
        at = slice(128 * i, 128 * (i + 1))
        new_table_ref[:, at] = table_ref[:, at] - grad_ref[:, at] * factor[i : i + 1]


def update(squares, state, table_t, grad_t):
    return pl.pallas_call(
        update_kernel,
        out_shape=(
            jax.ShapeDtypeStruct((WIDTH, TOUCH), F32),
            jax.ShapeDtypeStruct((TOUCH // 128, 128), F32),
        ),
        compiler_params=params(16),
        name="update",
    )(squares, state, table_t, grad_t)


def normalise(values):
    center = values - jnp.mean(values, axis=-1, keepdims=True)
    root = lax.rsqrt(jnp.mean(center * center, axis=-1, keepdims=True) + NORM_EPS)
    return center * root, root


def normalise_back(grad, normed, root):
    along = jnp.mean(grad * normed, axis=-1, keepdims=True)
    return root * (grad - jnp.mean(grad, axis=-1, keepdims=True) - normed * along)


def columns_of(row):
    return jnp.broadcast_to(row.astype(F32), (128, TOK_DEV)).T


def layer_kernel(
    member,
    received_ref,
    place_ref,
    segment_ref,
    w_ref,
    w_out_ref,
    cotangent_ref,
    out_ref,
    pieces_ref,
    slots_ref,
    segment_col,
    embedded_ref,
    normed_ref,
    gates_ref,
    slope_ref,
    values_ref,
    queries_ref,
    keys_ref,
    weights_ref,
    score_slope_ref,
    attended_ref,
    grad_attended_ref,
    grad_queries_ref,
    grad_u_ref,
    token_grad_ref,
):
    place = place_ref[pl.ds(member(), 1), :]
    segment_col[...] = columns_of(segment_ref[...])
    left = iota((HALF, 128), 1) < WIDTH
    four = 4 * HALF
    units = [
        (j, h, slice(BLOCK * j, min(TOK_DEV, BLOCK * j + REACH)), slice(BLOCK * j, BLOCK * (j + 1)), slice(HDIM * h, HDIM * (h + 1)))
        for j in range(TOK_DEV // BLOCK)
        for h in range(HEADS)
    ]

    def gather_slots(t, carry):
        parts = []
        for i in range(4):
            block = received_ref[4 * t + i].astype(F32)
            parts.append([block[HALF * c : HALF * (c + 1)] for c in range(COLS)])
        at = pl.multiple_of(four * t, four)
        for j in range(COLS // 2):
            pairs = [(part[2 * j], part[2 * j + 1]) for part in parts]
            first = [jnp.where(left, even, odd) for even, odd in pairs]
            second = [pltpu.roll(jnp.where(left, odd, even), WIDTH, 1) for even, odd in pairs]
            tile = slice(128 * j, 128 * (j + 1))
            slots_ref[pl.ds(at, four), tile] = jnp.concatenate(first, axis=0).astype(BF16)
            slots_ref[pl.ds(TABLES * HALF + at, four), tile] = jnp.concatenate(second, axis=0).astype(BF16)
        return carry

    lax.fori_loop(0, TABLES // 4, gather_slots, 0)

    at = columns_of(place).astype(I32)
    lane = iota((TOK_DEV, 128), 1)
    onehot = jnp.concatenate(
        [jnp.where(at == lane + 128 * j, 1.0, 0.0).astype(BF16) for j in range(TABLES * CAP // 128)],
        axis=1,
    )
    embedded = jnp.dot(onehot, slots_ref[...], preferred_element_type=F32)
    embedded_ref[...] = embedded.astype(BF16)
    normed, root = normalise(embedded)
    normed_ref[...] = normed.astype(BF16)
    piece = 256
    for p in range(4 * D // piece):
        part = slice(piece * p, piece * (p + 1))
        linear = 0.5 * jnp.dot(normed_ref[...], w_ref[:, part], preferred_element_type=F32)
        bend = jnp.tanh(linear)
        swish = linear + linear * bend
        gate = 0.5 + 0.5 * bend
        ref = (gates_ref, values_ref, queries_ref, keys_ref)[piece * p // D]
        within = piece * p % D
        ref[:, within : within + piece] = swish.astype(ref.dtype)
        slope_ref[:, part] = gate + swish * (1.0 - gate)

    scale = HDIM**-0.5
    attended_ref[...] = jnp.zeros_like(attended_ref)
    for j, h, rows, keys, head in units:
        length = rows.stop - rows.start
        allowed = segment_col[rows, :] == segment_ref[:, keys].astype(F32)
        allowed = allowed & (iota((length, BLOCK), 0) >= iota((length, BLOCK), 1))
        scores = nt_dot(queries_ref[rows, head], keys_ref[keys, head])
        scores = jnp.where(allowed, scores * (0.5 * scale), FAR)
        bend = jnp.tanh(scores)
        swish = scores + scores * bend
        gate = 0.5 + 0.5 * bend
        weights = swish.astype(BF16)
        weights_ref[HEADS * j + h, :, :length] = weights.T
        score_slope_ref[HEADS * j + h, :length, :] = scale * (gate + swish * (1.0 - gate))
        attended_ref[rows, head] += jnp.dot(weights, values_ref[keys, head], preferred_element_type=F32)

    again, root_again = normalise(attended_ref[...])
    gated = (again * gates_ref[...]).astype(BF16)
    out = jnp.dot(gated, w_out_ref[...], preferred_element_type=F32)
    out_ref[...] = (out + embedded_ref[...].astype(F32)).astype(BF16)
    grad_gated = nt_dot(cotangent_ref[...], w_out_ref[...]).astype(BF16).astype(F32)
    grad_u_ref[:, :D] = (grad_gated * again * slope_ref[:, :D]).astype(BF16)
    grad_attended_ref[...] = normalise_back(grad_gated * gates_ref[...], again, root_again).astype(BF16)

    grad_queries_ref[...] = jnp.zeros_like(grad_queries_ref)
    for j, h, rows, keys, head in units:
        length = rows.stop - rows.start
        grad_weights = nt_dot(grad_attended_ref[rows, head], values_ref[keys, head])
        grad_scores = (grad_weights * score_slope_ref[HEADS * j + h, :length, :]).astype(BF16)
        grad_queries_ref[rows, head] += jnp.dot(grad_scores, keys_ref[keys, head], preferred_element_type=F32)
        grad_values = jnp.dot(
            weights_ref[HEADS * j + h, :, :length], grad_attended_ref[rows, head], preferred_element_type=F32
        )
        grad_keys = tn_dot(grad_scores, queries_ref[rows, head])
        for k, grad in ((1, grad_values), (3, grad_keys)):
            part = slice(k * D + head.start, k * D + head.stop)
            grad_u_ref[keys, part] = (grad * slope_ref[keys, part]).astype(BF16)
    grad_u_ref[:, 2 * D : 3 * D] = (grad_queries_ref[...] * slope_ref[:, 2 * D : 3 * D]).astype(BF16)

    grad = nt_dot(grad_u_ref[...], w_ref[...])
    grad = normalise_back(grad, normed_ref[...].astype(F32), root)
    token_grad_ref[...] = (grad + cotangent_ref[...].astype(F32)).astype(BF16)

    onehot = jnp.where(place == iota((TABLES * CAP, TOK_DEV), 0), 1.0, 0.0).astype(BF16)
    half = TABLES * HALF
    for j in range(COLS // 2):
        if j % 2 == 0:
            part = slice(128 * j, 128 * (j + 2))
            sent = jnp.dot(onehot, token_grad_ref[:, part], preferred_element_type=F32)
        tile = slice(128 * (j % 2), 128 * (j % 2 + 1))
        first, second = sent[:half, tile], pltpu.roll(sent[half:, tile], WIDTH, 1)
        wide = iota((half, 128), 1) < WIDTH
        even, odd = jnp.where(wide, first, second), jnp.where(wide, second, first)
        for t in range(TABLES):
            rows = slice(HALF * t, HALF * (t + 1))
            pieces_ref[t, 2 * HALF * j : 2 * HALF * (j + 1), :] = jnp.concatenate(
                [even[rows], odd[rows]], axis=0
            ).astype(BF16)


def layer(received, place, member, segment, w_uvqk, w_out, cotangent):
    count = TOK_DEV // BLOCK * HEADS
    return pl.pallas_call(
        functools.partial(layer_kernel, member),
        out_shape=(
            jax.ShapeDtypeStruct((TOK_DEV, D), BF16),
            jax.ShapeDtypeStruct((TABLES, COLS * HALF, 128), BF16),
        ),
        scratch_shapes=[
            pltpu.VMEM((TABLES * CAP, D), BF16),
            pltpu.VMEM((TOK_DEV, 128), F32),
            pltpu.VMEM((TOK_DEV, D), BF16),
            pltpu.VMEM((TOK_DEV, D), BF16),
            pltpu.VMEM((TOK_DEV, D), F32),
            pltpu.VMEM((TOK_DEV, 4 * D), F32),
            pltpu.VMEM((TOK_DEV, D), BF16),
            pltpu.VMEM((TOK_DEV, D), BF16),
            pltpu.VMEM((TOK_DEV, D), BF16),
            pltpu.VMEM((count, BLOCK, REACH_TILES), BF16),
            pltpu.VMEM((count, REACH, BLOCK), F32),
            pltpu.VMEM((TOK_DEV, D), F32),
            pltpu.VMEM((TOK_DEV, D), BF16),
            pltpu.VMEM((TOK_DEV, D), F32),
            pltpu.VMEM((TOK_DEV, 4 * D), BF16),
            pltpu.VMEM((TOK_DEV, D), BF16),
        ],
        compiler_params=params(48),
        name="layer",
    )(received, place, segment, w_uvqk, w_out, cotangent)


def exchange(blocks):
    blocks = blocks.reshape(TABLES * COLS, HALF, 128)
    blocks = lax.all_to_all(blocks, ("table", "col"), split_axis=0, concat_axis=0, tiled=True)
    return blocks.reshape(TABLES, COLS * HALF, 128)


def shards(table_rows, ada_state, w_uvqk, w_out, tok_owner, tok_slot, seg_ids, cotangent):
    def member():
        return lax.axis_index("col")

    def parity():
        return lax.axis_index("col") % 2

    table_t = table_rows.T
    asks, place = make_asks(tok_owner.reshape(1, COLS * TOK_DEV), tok_slot)
    asked = lax.all_to_all(asks, "table", split_axis=0, concat_axis=0, tiled=True)
    received = exchange(pick_rows(asked, make_rows(table_t), parity))
    layer_out, pieces = layer(received, place, member, seg_ids, w_uvqk, w_out, cotangent)
    arrived = exchange(pieces)
    grad_t, squares = add_rows(asked, arrived, parity)
    squares = lax.all_to_all(squares, "col", split_axis=0, concat_axis=0, tiled=True)
    new_table_t, new_state = update(
        squares, ada_state.reshape(TOUCH // 128, 128), table_t, grad_t
    )
    return (layer_out, new_table_t.T, new_state.reshape(TOUCH))


def solution(mesh):
    in_specs = (
        P("table", "col"),
        P("table"),
        P(),
        P(),
        P("table", None, None),
        P("table", None),
        P(("table", "col"), None),
        P(("table", "col"), None),
    )
    out_specs = (P(("table", "col"), None), P("table", "col"), P("table"))
    return jax.shard_map(shards, mesh=mesh, in_specs=in_specs, out_specs=out_specs, check_vma=False)
```

```python
import functools

import jax
import jax.numpy as jnp
from jax import lax
from jax.experimental import pallas as pl
from jax.experimental.pallas import tpu as pltpu
from jax.sharding import PartitionSpec as P

D = 512
HEADS = 4
HDIM = 128
TOK_DEV = 640
TABLES = 16
COLS = 8
CAP = 80
HALF = CAP // 2
TOUCH = 2048
WIDTH = D // COLS
HI = 256
HI_BITS = 8
LO = TOUCH // HI
ASKS = 640
BLOCK = 128
REACH = 288
DEPTH = 2
PAIR = 2 * ASKS
REACH_TILES = 384
FAR = -1.0e4

NORM_EPS = 1e-05
ROOT_EPS = 1e-08
STEP_SIZE = 0.3

F32 = jnp.float32
BF16 = jnp.bfloat16
I32 = jnp.int32


def iota(shape, dim):
    return lax.broadcasted_iota(I32, shape, dim)


def nt_dot(a, b):
    return lax.dot_general(a, b, (((1,), (1,)), ((), ())), preferred_element_type=F32)


def tn_dot(a, b):
    return lax.dot_general(a, b, (((0,), (0,)), ((), ())), preferred_element_type=F32)


def params(megabytes):
    return pltpu.CompilerParams(vmem_limit_bytes=megabytes * 1024 * 1024)


def spans_of(row_ref):
    return [row_ref[:, TOK_DEV * m : TOK_DEV * (m + 1)] for m in range(COLS)]


def hits_of(owner_ref):
    table = iota((TABLES, TOK_DEV), 0)
    return [jnp.where(owner == table, 1.0, 0.0) for owner in spans_of(owner_ref)]


def ask_kernel(owner_ref, slot_ref, asks_ref, place_ref):
    lower = jnp.where(iota((TOK_DEV, TOK_DEV), 0) <= iota((TOK_DEV, TOK_DEV), 1), 1.0, 0.0).astype(BF16)
    hits = hits_of(owner_ref)
    running = jnp.dot(
        jnp.concatenate(hits, axis=0).astype(BF16), lower, preferred_element_type=F32
    )
    lane = iota((TABLES, 128), 1)
    slot_at = iota((128, TOK_DEV), 0)
    tiles = [jnp.zeros((TABLES, 128), F32) for _ in range(ASKS // 128)]
    members = zip(hits, spans_of(owner_ref), spans_of(slot_ref))
    for m, (hit, owner, slot) in enumerate(members):
        count = running[TABLES * m : TABLES * (m + 1)] * hit
        placing = jnp.sum(count, axis=0, keepdims=True).astype(I32) - 1
        onehot = jnp.where(slot_at == placing, 1.0, 0.0).astype(BF16)
        high = (slot >> HI_BITS).astype(F32) * hit
        low = (slot & (HI - 1)).astype(F32) * hit
        found = nt_dot(jnp.concatenate([high, low], axis=0).astype(BF16), onehot)
        value = found[:TABLES] * float(HI) + found[TABLES:]
        for h in range(2):
            begin = h * (ASKS // 2) + m * HALF
            moved = pltpu.roll(value, (begin - h * HALF) % 128, 1)
            for j in range(begin // 128, (begin + HALF - 1) // 128 + 1):
                at = lane + 128 * j
                tiles[j] = jnp.where((at >= begin) & (at < begin + HALF), moved, tiles[j])
        place_ref[m : m + 1, :] = (
            owner * HALF + placing + jnp.where(placing >= HALF, TABLES * HALF - HALF, 0)
        )
    for j, tile in enumerate(tiles):
        asks_ref[:, 0, 128 * j : 128 * (j + 1)] = tile.astype(I32)


def make_asks(owner, slot):
    return pl.pallas_call(
        ask_kernel,
        out_shape=(
            jax.ShapeDtypeStruct((TABLES, 1, ASKS), I32),
            jax.ShapeDtypeStruct((COLS, TOK_DEV), I32),
        ),
        compiler_params=params(16),
        name="ask",
    )(owner, slot)


def ask_pair(asks_ref, i):
    even, odd = asks_ref[2 * i], asks_ref[2 * i + 1]
    first = iota((1, ASKS), 1) < ASKS // 2
    low = jnp.where(first, even, pltpu.roll(odd, ASKS // 2, 1))
    high = jnp.where(first, pltpu.roll(even, ASKS // 2, 1), odd)
    return jnp.concatenate([low, high], axis=1)


def ask_onehot(ask):
    rows = iota((HI, PAIR), 0).astype(F32).astype(BF16)
    wanted = (ask & (HI - 1)).astype(F32).astype(BF16)
    return jnp.where(rows == wanted, jnp.ones((), BF16), jnp.zeros((), BF16))


def rows_kernel(table_ref, rows_ref):
    for lo in range(LO):
        rows_ref[WIDTH * lo : WIDTH * (lo + 1), :] = table_ref[:, HI * lo : HI * (lo + 1)].astype(BF16)


def make_rows(table_t):
    return pl.pallas_call(
        rows_kernel,
        out_shape=jax.ShapeDtypeStruct((LO * WIDTH, HI), BF16),
        compiler_params=params(8),
        name="rows",
    )(table_t)


def pick_kernel(parity, asks_ref, rows_ref, reply_ref):
    par = parity()

    def two_groups(i, carry):
        ask = ask_pair(asks_ref, i)
        found = jnp.dot(rows_ref[...], ask_onehot(ask), preferred_element_type=F32)
        low = jnp.broadcast_to(ask >> HI_BITS, (WIDTH, PAIR))
        parts = [found[WIDTH * lo : WIDTH * (lo + 1)] for lo in range(LO)]
        for bit in (1, 2, 4):
            upper = (low & bit) != 0
            parts = [jnp.where(upper, parts[i + 1], parts[i]) for i in range(0, len(parts), 2)]
        kept = parts[0]
        first, second = kept[:, :ASKS], kept[:, ASKS:]
        stacked = jnp.concatenate(
            [jnp.where(par == 0, first, second), jnp.where(par == 0, second, first)], axis=0
        )
        replies = stacked.T.astype(BF16)
        reply_ref[2 * i] = replies[: COLS * HALF]
        reply_ref[2 * i + 1] = replies[COLS * HALF :]
        return carry

    lax.fori_loop(0, TABLES // 2, two_groups, 0, unroll=8)


def pick_rows(asks, rows, parity):
    return pl.pallas_call(
        functools.partial(pick_kernel, parity),
        out_shape=jax.ShapeDtypeStruct((TABLES, COLS * HALF, 128), BF16),
        compiler_params=params(32),
        name="pick",
    )(asks, rows)


def add_kernel(parity, asks_ref, arrived_ref, grad_ref, squares_ref, total_ref):
    par = parity()
    total_ref[...] = jnp.zeros_like(total_ref)

    def two_groups(i, carry):
        ask = ask_pair(asks_ref, i)
        block = jnp.concatenate([arrived_ref[2 * i], arrived_ref[2 * i + 1]], axis=0).astype(F32).T
        upper, lower = block[:WIDTH], block[WIDTH:]
        slots = jnp.concatenate(
            [jnp.where(par == 0, upper, lower), jnp.where(par == 0, lower, upper)], axis=1
        )
        low = jnp.broadcast_to(ask >> HI_BITS, (WIDTH, PAIR))
        spread = jnp.concatenate(
            [jnp.where(low == lo, slots, 0.0).astype(BF16) for lo in range(LO)], axis=0
        )
        total_ref[...] += nt_dot(spread, ask_onehot(ask))
        return carry

    lax.fori_loop(0, TABLES // 2, two_groups, 0, unroll=8)
    sums = []
    for lo in range(LO):
        part = total_ref[WIDTH * lo : WIDTH * (lo + 1), :]
        grad_ref[:, HI * lo : HI * (lo + 1)] = part
        square = jnp.sum(part * part, axis=0, keepdims=True)
        sums += [square[:, :128], square[:, 128:]]
    squares_ref[...] = jnp.concatenate(sums, axis=0)


def add_rows(asks, arrived, parity):
    return pl.pallas_call(
        functools.partial(add_kernel, parity),
        out_shape=(
            jax.ShapeDtypeStruct((WIDTH, TOUCH), F32),
            jax.ShapeDtypeStruct((TOUCH // 128, 128), F32),
        ),
        scratch_shapes=[pltpu.VMEM((LO * WIDTH, HI), F32)],
        compiler_params=params(48),
        name="add",
    )(asks, arrived)


def update_kernel(own_ref, near_ref, far_ref, last_ref, state_ref, table_ref, grad_ref, new_table_ref, new_state_ref):
    squares = (own_ref[...] + near_ref[...]) + (far_ref[...] + last_ref[...])
    state = state_ref[...] + squares / D
    new_state_ref[...] = state
    factor = STEP_SIZE / (jnp.sqrt(state) + ROOT_EPS)
    for i in range(TOUCH // 128):
        at = slice(128 * i, 128 * (i + 1))
        new_table_ref[:, at] = table_ref[:, at] - grad_ref[:, at] * factor[i : i + 1]


def update(squares, state, table_t, grad_t):
    return pl.pallas_call(
        update_kernel,
        out_shape=(
            jax.ShapeDtypeStruct((WIDTH, TOUCH), F32),
            jax.ShapeDtypeStruct((TOUCH // 128, 128), F32),
        ),
        compiler_params=params(16),
        name="update",
    )(*squares, state, table_t, grad_t)


def normalise(values):
    center = values - jnp.mean(values, axis=-1, keepdims=True)
    root = lax.rsqrt(jnp.mean(center * center, axis=-1, keepdims=True) + NORM_EPS)
    return center * root, root


def normalise_back(grad, normed, root):
    along = jnp.mean(grad * normed, axis=-1, keepdims=True)
    return root * (grad - jnp.mean(grad, axis=-1, keepdims=True) - normed * along)


def columns_of(row):
    return jnp.broadcast_to(row.astype(F32), (128, TOK_DEV)).T


def layer_kernel(
    member,
    received_ref,
    place_ref,
    segment_ref,
    w_ref,
    w_out_ref,
    cotangent_ref,
    out_ref,
    pieces_ref,
    slots_ref,
    segment_col,
    embedded_ref,
    normed_ref,
    gates_ref,
    slope_ref,
    values_ref,
    queries_ref,
    keys_ref,
    weights_ref,
    score_slope_ref,
    attended_ref,
    grad_attended_ref,
    grad_queries_ref,
    grad_u_ref,
    token_grad_ref,
):
    place = place_ref[pl.ds(member(), 1), :]
    segment_col[...] = columns_of(segment_ref[...])
    left = iota((HALF, 128), 1) < WIDTH
    four = 4 * HALF
    units = [
        (j, h, slice(BLOCK * j, min(TOK_DEV, BLOCK * j + REACH)), slice(BLOCK * j, BLOCK * (j + 1)), slice(HDIM * h, HDIM * (h + 1)))
        for j in range(TOK_DEV // BLOCK)
        for h in range(HEADS)
    ]

    def gather_slots(t, carry):
        parts = []
        for i in range(4):
            block = received_ref[4 * t + i].astype(F32)
            parts.append([block[HALF * c : HALF * (c + 1)] for c in range(COLS)])
        at = four * t
        for j in range(COLS // 2):
            pairs = [(part[2 * j], part[2 * j + 1]) for part in parts]
            first = [jnp.where(left, even, odd) for even, odd in pairs]
            second = [pltpu.roll(jnp.where(left, odd, even), WIDTH, 1) for even, odd in pairs]
            tile = slice(128 * j, 128 * (j + 1))
            slots_ref[slice(at, at + four), tile] = jnp.concatenate(first, axis=0).astype(BF16)
            slots_ref[slice(TABLES * HALF + at, TABLES * HALF + at + four), tile] = jnp.concatenate(second, axis=0).astype(BF16)
        return carry

    for t in range(TABLES // 4):
        gather_slots(t, 0)

    at = columns_of(place).astype(I32)
    lane = iota((TOK_DEV, 128), 1)
    onehot = jnp.concatenate(
        [jnp.where(at == lane + 128 * j, 1.0, 0.0).astype(BF16) for j in range(TABLES * CAP // 128)],
        axis=1,
    )
    embedded = jnp.dot(onehot, slots_ref[...], preferred_element_type=F32)
    embedded_ref[...] = embedded.astype(BF16)
    normed, root = normalise(embedded)
    normed_ref[...] = normed.astype(BF16)
    piece = 256
    def project(p):
        return jnp.dot(
            normed_ref[...], w_ref[:, piece * p : piece * (p + 1)], preferred_element_type=F32
        )

    ahead = project(0)
    for p in range(4 * D // piece):
        part = slice(piece * p, piece * (p + 1))
        linear = 0.5 * ahead
        if p + 1 < 4 * D // piece:
            ahead = project(p + 1)
        bend = jnp.tanh(linear)
        swish = linear + linear * bend
        gate = 0.5 + 0.5 * bend
        ref = (gates_ref, values_ref, queries_ref, keys_ref)[piece * p // D]
        within = piece * p % D
        ref[:, within : within + piece] = swish.astype(ref.dtype)
        slope_ref[:, part] = gate + swish * (1.0 - gate)

    scale = HDIM**-0.5
    attended_ref[...] = jnp.zeros_like(attended_ref)
    def score(unit):
        j, h, rows, keys, head = unit
        return nt_dot(queries_ref[rows, head], keys_ref[keys, head])

    ahead = [score(units[u]) for u in range(DEPTH)]
    for u, (j, h, rows, keys, head) in enumerate(units):
        length = rows.stop - rows.start
        allowed = segment_col[rows, :] == segment_ref[:, keys].astype(F32)
        allowed = allowed & (iota((length, BLOCK), 0) >= iota((length, BLOCK), 1))
        scores = ahead.pop(0)
        if u + DEPTH < len(units):
            ahead.append(score(units[u + DEPTH]))
        scores = jnp.where(allowed, scores * (0.5 * scale), FAR)
        bend = jnp.tanh(scores)
        swish = scores + scores * bend
        gate = 0.5 + 0.5 * bend
        weights = swish.astype(BF16)
        weights_ref[HEADS * j + h, :, :length] = weights.T
        score_slope_ref[HEADS * j + h, :length, :] = scale * (gate + swish * (1.0 - gate))
        attended_ref[rows, head] += jnp.dot(weights, values_ref[keys, head], preferred_element_type=F32)

    again, root_again = normalise(attended_ref[...])
    gated = (again * gates_ref[...]).astype(BF16)
    out = jnp.dot(gated, w_out_ref[...], preferred_element_type=F32)
    out_ref[...] = (out + embedded_ref[...].astype(F32)).astype(BF16)
    grad_gated = nt_dot(cotangent_ref[...], w_out_ref[...]).astype(BF16).astype(F32)
    grad_u_ref[:, :D] = (grad_gated * again * slope_ref[:, :D]).astype(BF16)
    grad_attended_ref[...] = normalise_back(grad_gated * gates_ref[...], again, root_again).astype(BF16)

    grad_queries_ref[...] = jnp.zeros_like(grad_queries_ref)
    def weigh_back(unit):
        j, h, rows, keys, head = unit
        return nt_dot(grad_attended_ref[rows, head], values_ref[keys, head])

    ahead = [weigh_back(units[u]) for u in range(DEPTH)]
    for u, (j, h, rows, keys, head) in enumerate(units):
        length = rows.stop - rows.start
        grad_weights = ahead.pop(0)
        if u + DEPTH < len(units):
            ahead.append(weigh_back(units[u + DEPTH]))
        grad_scores = (grad_weights * score_slope_ref[HEADS * j + h, :length, :]).astype(BF16)
        grad_queries_ref[rows, head] += jnp.dot(grad_scores, keys_ref[keys, head], preferred_element_type=F32)
        grad_values = jnp.dot(
            weights_ref[HEADS * j + h, :, :length], grad_attended_ref[rows, head], preferred_element_type=F32
        )
        grad_keys = tn_dot(grad_scores, queries_ref[rows, head])
        for k, grad in ((1, grad_values), (3, grad_keys)):
            part = slice(k * D + head.start, k * D + head.stop)
            grad_u_ref[keys, part] = (grad * slope_ref[keys, part]).astype(BF16)
    grad_u_ref[:, 2 * D : 3 * D] = (grad_queries_ref[...] * slope_ref[:, 2 * D : 3 * D]).astype(BF16)

    grad = nt_dot(grad_u_ref[...], w_ref[...])
    grad = normalise_back(grad, normed_ref[...].astype(F32), root)
    token_grad_ref[...] = (grad + cotangent_ref[...].astype(F32)).astype(BF16)

    onehot = jnp.where(place == iota((TABLES * CAP, TOK_DEV), 0), 1.0, 0.0).astype(BF16)
    half = TABLES * HALF
    for j in range(COLS // 2):
        if j % 2 == 0:
            part = slice(128 * j, 128 * (j + 2))
            sent = jnp.dot(onehot, token_grad_ref[:, part], preferred_element_type=F32)
        tile = slice(128 * (j % 2), 128 * (j % 2 + 1))
        first, second = sent[:half, tile], pltpu.roll(sent[half:, tile], WIDTH, 1)
        wide = iota((half, 128), 1) < WIDTH
        even, odd = jnp.where(wide, first, second), jnp.where(wide, second, first)
        for t in range(TABLES):
            rows = slice(HALF * t, HALF * (t + 1))
            pieces_ref[t, 2 * HALF * j : 2 * HALF * (j + 1), :] = jnp.concatenate(
                [even[rows], odd[rows]], axis=0
            ).astype(BF16)


def layer(received, place, member, segment, w_uvqk, w_out, cotangent):
    count = TOK_DEV // BLOCK * HEADS
    return pl.pallas_call(
        functools.partial(layer_kernel, member),
        out_shape=(
            jax.ShapeDtypeStruct((TOK_DEV, D), BF16),
            jax.ShapeDtypeStruct((TABLES, COLS * HALF, 128), BF16),
        ),
        scratch_shapes=[
            pltpu.VMEM((TABLES * CAP, D), BF16),
            pltpu.VMEM((TOK_DEV, 128), F32),
            pltpu.VMEM((TOK_DEV, D), BF16),
            pltpu.VMEM((TOK_DEV, D), BF16),
            pltpu.VMEM((TOK_DEV, D), F32),
            pltpu.VMEM((TOK_DEV, 4 * D), F32),
            pltpu.VMEM((TOK_DEV, D), BF16),
            pltpu.VMEM((TOK_DEV, D), BF16),
            pltpu.VMEM((TOK_DEV, D), BF16),
            pltpu.VMEM((count, BLOCK, REACH_TILES), BF16),
            pltpu.VMEM((count, REACH, BLOCK), F32),
            pltpu.VMEM((TOK_DEV, D), F32),
            pltpu.VMEM((TOK_DEV, D), BF16),
            pltpu.VMEM((TOK_DEV, D), F32),
            pltpu.VMEM((TOK_DEV, 4 * D), BF16),
            pltpu.VMEM((TOK_DEV, D), BF16),
        ],
        compiler_params=params(48),
        name="layer",
    )(received, place, segment, w_uvqk, w_out, cotangent)


def exchange(blocks):
    blocks = blocks.reshape(TABLES * COLS, HALF, 128)
    blocks = lax.all_to_all(blocks, ("table", "col"), split_axis=0, concat_axis=0, tiled=True)
    return blocks.reshape(TABLES, COLS * HALF, 128)


def swap_cols(values, mask):
    return lax.ppermute(values, "col", [(c, c ^ mask) for c in range(COLS)])


def shards(table_rows, ada_state, w_uvqk, w_out, tok_owner, tok_slot, seg_ids, cotangent):
    def member():
        return lax.axis_index("col")

    def parity():
        return lax.axis_index("col") % 2

    table_t = table_rows.T
    asks, place = make_asks(tok_owner.reshape(1, COLS * TOK_DEV), tok_slot)
    asked = lax.all_to_all(asks, "table", split_axis=0, concat_axis=0, tiled=True)
    received = exchange(pick_rows(asked, make_rows(table_t), parity))
    layer_out, pieces = layer(received, place, member, seg_ids, w_uvqk, w_out, cotangent)
    arrived = exchange(pieces)
    grad_t, squares = add_rows(asked, arrived, parity)
    squares = squares + swap_cols(squares, 1)
    squares = [squares] + [swap_cols(squares, 2 * k) for k in range(1, COLS // 2)]
    new_table_t, new_state = update(
        squares, ada_state.reshape(TOUCH // 128, 128), table_t, grad_t
    )
    return (layer_out, new_table_t.T, new_state.reshape(TOUCH))


def solution(mesh):
    in_specs = (
        P("table", "col"),
        P("table"),
        P(),
        P(),
        P("table", None, None),
        P("table", None),
        P(("table", "col"), None),
        P(("table", "col"), None),
    )
    out_specs = (P(("table", "col"), None), P("table", "col"), P("table"))
    return jax.shard_map(shards, mesh=mesh, in_specs=in_specs, out_specs=out_specs, check_vma=False)
```

```python
import functools

import jax
import jax.numpy as jnp
from jax import lax
from jax.experimental import pallas as pl
from jax.experimental.pallas import tpu as pltpu
from jax.sharding import PartitionSpec as P

D = 512
HEADS = 4
HDIM = 128
TOK_DEV = 640
TABLES = 16
COLS = 8
CAP = 80
HALF = CAP // 2
TOUCH = 2048
WIDTH = D // COLS
HI = 256
HI_BITS = 8
LO = TOUCH // HI
ASKS = 640
BLOCK = 128
REACH = 288
DEPTH = 2
PAIR = 2 * ASKS
REACH_TILES = 384
FAR = -64.0

NORM_EPS = 1e-05
ROOT_EPS = 1e-08
STEP_SIZE = 0.3

F32 = jnp.float32
BF16 = jnp.bfloat16
I32 = jnp.int32


def iota(shape, dim):
    return lax.broadcasted_iota(I32, shape, dim)


def nt_dot(a, b):
    return lax.dot_general(a, b, (((1,), (1,)), ((), ())), preferred_element_type=F32)


def tn_dot(a, b):
    return lax.dot_general(a, b, (((0,), (0,)), ((), ())), preferred_element_type=F32)


def params(megabytes):
    return pltpu.CompilerParams(vmem_limit_bytes=megabytes * 1024 * 1024)


def spans_of(row_ref):
    return [row_ref[:, TOK_DEV * m : TOK_DEV * (m + 1)] for m in range(COLS)]


def hits_of(owner_ref):
    table = iota((TABLES, TOK_DEV), 0)
    return [jnp.where(owner == table, 1.0, 0.0) for owner in spans_of(owner_ref)]


def ask_kernel(owner_ref, slot_ref, asks_ref, place_ref):
    lower = jnp.where(iota((TOK_DEV, TOK_DEV), 0) <= iota((TOK_DEV, TOK_DEV), 1), 1.0, 0.0).astype(BF16)
    hits = hits_of(owner_ref)
    running = jnp.dot(
        jnp.concatenate(hits, axis=0).astype(BF16), lower, preferred_element_type=F32
    )
    lane = iota((TABLES, 128), 1)
    slot_at = iota((128, TOK_DEV), 0)
    tiles = [jnp.zeros((TABLES, 128), F32) for _ in range(ASKS // 128)]
    members = zip(hits, spans_of(owner_ref), spans_of(slot_ref))
    for m, (hit, owner, slot) in enumerate(members):
        count = running[TABLES * m : TABLES * (m + 1)] * hit
        placing = jnp.sum(count, axis=0, keepdims=True).astype(I32) - 1
        onehot = jnp.where(slot_at == placing, 1.0, 0.0).astype(BF16)
        high = (slot >> HI_BITS).astype(F32) * hit
        low = (slot & (HI - 1)).astype(F32) * hit
        found = nt_dot(jnp.concatenate([high, low], axis=0).astype(BF16), onehot)
        value = found[:TABLES] * float(HI) + found[TABLES:]
        for h in range(2):
            begin = h * (ASKS // 2) + m * HALF
            moved = pltpu.roll(value, (begin - h * HALF) % 128, 1)
            for j in range(begin // 128, (begin + HALF - 1) // 128 + 1):
                at = lane + 128 * j
                tiles[j] = jnp.where((at >= begin) & (at < begin + HALF), moved, tiles[j])
        place_ref[m : m + 1, :] = (
            owner * HALF + placing + jnp.where(placing >= HALF, TABLES * HALF - HALF, 0)
        )
    for j, tile in enumerate(tiles):
        asks_ref[:, 0, 128 * j : 128 * (j + 1)] = tile.astype(I32)


def make_asks(owner, slot):
    return pl.pallas_call(
        ask_kernel,
        out_shape=(
            jax.ShapeDtypeStruct((TABLES, 1, ASKS), I32),
            jax.ShapeDtypeStruct((COLS, TOK_DEV), I32),
        ),
        name="ask",
    )(owner, slot)


def ask_pair(asks_ref, i):
    even, odd = asks_ref[2 * i], asks_ref[2 * i + 1]
    first = iota((1, ASKS), 1) < ASKS // 2
    low = jnp.where(first, even, pltpu.roll(odd, ASKS // 2, 1))
    high = jnp.where(first, pltpu.roll(even, ASKS // 2, 1), odd)
    return jnp.concatenate([low, high], axis=1)


def ask_onehot(ask):
    rows = iota((HI, PAIR), 0).astype(F32).astype(BF16)
    wanted = (ask & (HI - 1)).astype(F32).astype(BF16)
    return jnp.where(rows == wanted, jnp.ones((), BF16), jnp.zeros((), BF16))


def rows_kernel(table_ref, rows_ref):
    for lo in range(LO):
        rows_ref[WIDTH * lo : WIDTH * (lo + 1), :] = table_ref[:, HI * lo : HI * (lo + 1)].astype(BF16)


def make_rows(table_t):
    return pl.pallas_call(
        rows_kernel,
        out_shape=jax.ShapeDtypeStruct((LO * WIDTH, HI), BF16),
        compiler_params=params(8),
        name="rows",
    )(table_t)


def pick_kernel(parity, asks_ref, rows_ref, reply_ref):
    par = parity()

    def two_groups(i, carry):
        ask = ask_pair(asks_ref, i)
        found = jnp.dot(rows_ref[...], ask_onehot(ask), preferred_element_type=F32)
        low = jnp.broadcast_to(ask >> HI_BITS, (WIDTH, PAIR))
        parts = [found[WIDTH * lo : WIDTH * (lo + 1)] for lo in range(LO)]
        for bit in (1, 2, 4):
            upper = (low & bit) != 0
            parts = [jnp.where(upper, parts[i + 1], parts[i]) for i in range(0, len(parts), 2)]
        kept = parts[0]
        first, second = kept[:, :ASKS], kept[:, ASKS:]
        stacked = jnp.concatenate(
            [jnp.where(par == 0, first, second), jnp.where(par == 0, second, first)], axis=0
        )
        replies = stacked.T.astype(BF16)
        reply_ref[2 * i] = replies[: COLS * HALF]
        reply_ref[2 * i + 1] = replies[COLS * HALF :]
        return carry

    lax.fori_loop(0, TABLES // 2, two_groups, 0, unroll=8)


def pick_rows(asks, rows, parity):
    return pl.pallas_call(
        functools.partial(pick_kernel, parity),
        out_shape=jax.ShapeDtypeStruct((TABLES, COLS * HALF, 128), BF16),
        compiler_params=params(32),
        name="pick",
    )(asks, rows)


def add_kernel(parity, asks_ref, arrived_ref, grad_ref, squares_ref, total_ref):
    par = parity()
    total_ref[...] = jnp.zeros_like(total_ref)

    def two_groups(i, carry):
        ask = ask_pair(asks_ref, i)
        block = jnp.concatenate([arrived_ref[2 * i], arrived_ref[2 * i + 1]], axis=0).astype(F32).T
        upper, lower = block[:WIDTH], block[WIDTH:]
        slots = jnp.concatenate(
            [jnp.where(par == 0, upper, lower), jnp.where(par == 0, lower, upper)], axis=1
        )
        low = jnp.broadcast_to(ask >> HI_BITS, (WIDTH, PAIR))
        spread = jnp.concatenate(
            [jnp.where(low == lo, slots, 0.0).astype(BF16) for lo in range(LO)], axis=0
        )
        total_ref[...] += nt_dot(spread, ask_onehot(ask))
        return carry

    lax.fori_loop(0, TABLES // 2, two_groups, 0, unroll=8)
    sums = []
    for lo in range(LO):
        part = total_ref[WIDTH * lo : WIDTH * (lo + 1), :]
        grad_ref[:, HI * lo : HI * (lo + 1)] = part
        square = jnp.sum(part * part, axis=0, keepdims=True)
        sums += [square[:, :128], square[:, 128:]]
    squares_ref[...] = jnp.concatenate(sums, axis=0)


def add_rows(asks, arrived, parity):
    return pl.pallas_call(
        functools.partial(add_kernel, parity),
        out_shape=(
            jax.ShapeDtypeStruct((WIDTH, TOUCH), F32),
            jax.ShapeDtypeStruct((TOUCH // 128, 128), F32),
        ),
        scratch_shapes=[pltpu.VMEM((LO * WIDTH, HI), F32)],
        compiler_params=params(48),
        name="add",
    )(asks, arrived)


def update_kernel(own_ref, near_ref, far_ref, last_ref, state_ref, table_ref, grad_ref, new_table_ref, new_state_ref):
    squares = (own_ref[...] + near_ref[...]) + (far_ref[...] + last_ref[...])
    state = state_ref[...] + squares / D
    new_state_ref[...] = state
    factor = STEP_SIZE / (jnp.sqrt(state) + ROOT_EPS)
    for i in range(TOUCH // 128):
        at = slice(128 * i, 128 * (i + 1))
        new_table_ref[:, at] = table_ref[:, at] - grad_ref[:, at] * factor[i : i + 1]


def update(squares, state, table_t, grad_t):
    return pl.pallas_call(
        update_kernel,
        out_shape=(
            jax.ShapeDtypeStruct((WIDTH, TOUCH), F32),
            jax.ShapeDtypeStruct((TOUCH // 128, 128), F32),
        ),
        compiler_params=params(16),
        name="update",
    )(*squares, state, table_t, grad_t)


def normalise(values):
    center = values - jnp.mean(values, axis=-1, keepdims=True)
    root = lax.rsqrt(jnp.mean(center * center, axis=-1, keepdims=True) + NORM_EPS)
    return center * root, root


def normalise_back(grad, normed, root):
    along = jnp.mean(grad * normed, axis=-1, keepdims=True)
    return root * (grad - jnp.mean(grad, axis=-1, keepdims=True) - normed * along)


def columns_of(row):
    return jnp.broadcast_to(row.astype(F32), (128, TOK_DEV)).T


def layer_kernel(
    member,
    received_ref,
    place_ref,
    segment_ref,
    w_ref,
    w_out_ref,
    cotangent_ref,
    out_ref,
    pieces_ref,
    slots_ref,
    segment_col,
    embedded_ref,
    normed_ref,
    gates_ref,
    slope_ref,
    values_ref,
    queries_ref,
    keys_ref,
    weights_ref,
    score_slope_ref,
    attended_ref,
    grad_attended_ref,
    grad_queries_ref,
    grad_u_ref,
    token_grad_ref,
):
    place = place_ref[pl.ds(member(), 1), :]
    segment_col[...] = columns_of(segment_ref[...])
    left = iota((HALF, 128), 1) < WIDTH
    four = 4 * HALF
    units = [
        (j, h, slice(BLOCK * j, min(TOK_DEV, BLOCK * j + REACH)), slice(BLOCK * j, BLOCK * (j + 1)), slice(HDIM * h, HDIM * (h + 1)))
        for j in range(TOK_DEV // BLOCK)
        for h in range(HEADS)
    ]

    def gather_slots(t, carry):
        parts = []
        for i in range(4):
            block = received_ref[4 * t + i].astype(F32)
            parts.append([block[HALF * c : HALF * (c + 1)] for c in range(COLS)])
        at = four * t
        for j in range(COLS // 2):
            pairs = [(part[2 * j], part[2 * j + 1]) for part in parts]
            first = [jnp.where(left, even, odd) for even, odd in pairs]
            second = [pltpu.roll(jnp.where(left, odd, even), WIDTH, 1) for even, odd in pairs]
            tile = slice(128 * j, 128 * (j + 1))
            slots_ref[slice(at, at + four), tile] = jnp.concatenate(first, axis=0).astype(BF16)
            slots_ref[slice(TABLES * HALF + at, TABLES * HALF + at + four), tile] = jnp.concatenate(second, axis=0).astype(BF16)
        return carry

    for t in range(TABLES // 4):
        gather_slots(t, 0)

    at = columns_of(place).astype(I32)
    lane = iota((TOK_DEV, 128), 1)
    onehot = jnp.concatenate(
        [jnp.where(at == lane + 128 * j, 1.0, 0.0).astype(BF16) for j in range(TABLES * CAP // 128)],
        axis=1,
    )
    embedded = jnp.dot(onehot, slots_ref[...], preferred_element_type=F32)
    embedded_ref[...] = embedded.astype(BF16)
    normed, root = normalise(embedded)
    normed_ref[...] = normed.astype(BF16)
    piece = 256
    def project(p):
        return jnp.dot(
            normed_ref[...], w_ref[:, piece * p : piece * (p + 1)], preferred_element_type=F32
        )

    ahead = project(0)
    for p in range(4 * D // piece):
        part = slice(piece * p, piece * (p + 1))
        linear = 0.5 * ahead
        if p + 1 < 4 * D // piece:
            ahead = project(p + 1)
        bend = jnp.tanh(linear)
        swish = linear + linear * bend
        gate = 0.5 + 0.5 * bend
        ref = (gates_ref, values_ref, queries_ref, keys_ref)[piece * p // D]
        within = piece * p % D
        ref[:, within : within + piece] = swish.astype(ref.dtype)
        slope_ref[:, part] = gate + swish * (1.0 - gate)

    scale = HDIM**-0.5
    attended_ref[...] = jnp.zeros_like(attended_ref)
    def score(unit):
        j, h, rows, keys, head = unit
        return nt_dot(queries_ref[rows, head], keys_ref[keys, head])

    ahead = [score(units[u]) for u in range(DEPTH)]
    for u, (j, h, rows, keys, head) in enumerate(units):
        length = rows.stop - rows.start
        allowed = segment_col[rows, :] == segment_ref[:, keys].astype(F32)
        allowed = allowed & (iota((length, BLOCK), 0) >= iota((length, BLOCK), 1))
        scores = ahead.pop(0)
        if u + DEPTH < len(units):
            ahead.append(score(units[u + DEPTH]))
        scores = jnp.where(allowed, scores * (0.5 * scale), FAR)
        bend = jnp.tanh(scores)
        swish = scores + scores * bend
        gate = 0.5 + 0.5 * bend
        weights = swish.astype(BF16)
        weights_ref[HEADS * j + h, :, :length] = weights.T
        score_slope_ref[HEADS * j + h, :length, :] = scale * (gate + swish * (1.0 - gate))
        attended_ref[rows, head] += jnp.dot(weights, values_ref[keys, head], preferred_element_type=F32)

    again, root_again = normalise(attended_ref[...])
    gated = (again * gates_ref[...]).astype(BF16)
    out = jnp.dot(gated, w_out_ref[...], preferred_element_type=F32)
    out_ref[...] = (out + embedded_ref[...].astype(F32)).astype(BF16)
    grad_gated = nt_dot(cotangent_ref[...], w_out_ref[...]).astype(BF16).astype(F32)
    grad_u_ref[:, :D] = (grad_gated * again * slope_ref[:, :D]).astype(BF16)
    grad_attended_ref[...] = normalise_back(grad_gated * gates_ref[...], again, root_again).astype(BF16)

    grad_queries_ref[...] = jnp.zeros_like(grad_queries_ref)
    def weigh_back(unit):
        j, h, rows, keys, head = unit
        return nt_dot(grad_attended_ref[rows, head], values_ref[keys, head])

    ahead = [weigh_back(units[u]) for u in range(DEPTH)]
    for u, (j, h, rows, keys, head) in enumerate(units):
        length = rows.stop - rows.start
        grad_weights = ahead.pop(0)
        if u + DEPTH < len(units):
            ahead.append(weigh_back(units[u + DEPTH]))
        grad_scores = (grad_weights * score_slope_ref[HEADS * j + h, :length, :]).astype(BF16)
        grad_queries_ref[rows, head] += jnp.dot(grad_scores, keys_ref[keys, head], preferred_element_type=F32)
        grad_values = jnp.dot(
            weights_ref[HEADS * j + h, :, :length], grad_attended_ref[rows, head], preferred_element_type=F32
        )
        grad_keys = tn_dot(grad_scores, queries_ref[rows, head])
        for k, grad in ((1, grad_values), (3, grad_keys)):
            part = slice(k * D + head.start, k * D + head.stop)
            grad_u_ref[keys, part] = (grad * slope_ref[keys, part]).astype(BF16)
    grad_u_ref[:, 2 * D : 3 * D] = (grad_queries_ref[...] * slope_ref[:, 2 * D : 3 * D]).astype(BF16)

    grad = nt_dot(grad_u_ref[...], w_ref[...])
    grad = normalise_back(grad, normed_ref[...].astype(F32), root)
    token_grad_ref[...] = (grad + cotangent_ref[...].astype(F32)).astype(BF16)

    onehot = jnp.where(place == iota((TABLES * CAP, TOK_DEV), 0), 1.0, 0.0).astype(BF16)
    half = TABLES * HALF
    for j in range(COLS // 2):
        if j % 2 == 0:
            part = slice(128 * j, 128 * (j + 2))
            sent = jnp.dot(onehot, token_grad_ref[:, part], preferred_element_type=F32)
        tile = slice(128 * (j % 2), 128 * (j % 2 + 1))
        first, second = sent[:half, tile], pltpu.roll(sent[half:, tile], WIDTH, 1)
        wide = iota((half, 128), 1) < WIDTH
        even, odd = jnp.where(wide, first, second), jnp.where(wide, second, first)
        for t in range(TABLES):
            rows = slice(HALF * t, HALF * (t + 1))
            pieces_ref[t, 2 * HALF * j : 2 * HALF * (j + 1), :] = jnp.concatenate(
                [even[rows], odd[rows]], axis=0
            ).astype(BF16)


def layer(received, place, member, segment, w_uvqk, w_out, cotangent):
    count = TOK_DEV // BLOCK * HEADS
    return pl.pallas_call(
        functools.partial(layer_kernel, member),
        out_shape=(
            jax.ShapeDtypeStruct((TOK_DEV, D), BF16),
            jax.ShapeDtypeStruct((TABLES, COLS * HALF, 128), BF16),
        ),
        scratch_shapes=[
            pltpu.VMEM((TABLES * CAP, D), BF16),
            pltpu.VMEM((TOK_DEV, 128), F32),
            pltpu.VMEM((TOK_DEV, D), BF16),
            pltpu.VMEM((TOK_DEV, D), BF16),
            pltpu.VMEM((TOK_DEV, D), F32),
            pltpu.VMEM((TOK_DEV, 4 * D), F32),
            pltpu.VMEM((TOK_DEV, D), BF16),
            pltpu.VMEM((TOK_DEV, D), BF16),
            pltpu.VMEM((TOK_DEV, D), BF16),
            pltpu.VMEM((count, BLOCK, REACH_TILES), BF16),
            pltpu.VMEM((count, REACH, BLOCK), F32),
            pltpu.VMEM((TOK_DEV, D), F32),
            pltpu.VMEM((TOK_DEV, D), BF16),
            pltpu.VMEM((TOK_DEV, D), F32),
            pltpu.VMEM((TOK_DEV, 4 * D), BF16),
            pltpu.VMEM((TOK_DEV, D), BF16),
        ],
        compiler_params=params(48),
        name="layer",
    )(received, place, segment, w_uvqk, w_out, cotangent)


def exchange(blocks):
    blocks = blocks.reshape(TABLES * COLS, HALF, 128)
    blocks = lax.all_to_all(blocks, ("table", "col"), split_axis=0, concat_axis=0, tiled=True)
    return blocks.reshape(TABLES, COLS * HALF, 128)


def swap_cols(values, mask):
    return lax.ppermute(values, "col", [(c, c ^ mask) for c in range(COLS)])


def shards(table_rows, ada_state, w_uvqk, w_out, tok_owner, tok_slot, seg_ids, cotangent):
    def member():
        return lax.axis_index("col")

    def parity():
        return lax.axis_index("col") % 2

    table_t = table_rows.T
    asks, place = make_asks(tok_owner.reshape(1, COLS * TOK_DEV), tok_slot)
    asked = lax.all_to_all(asks, "table", split_axis=0, concat_axis=0, tiled=True)
    received = exchange(pick_rows(asked, make_rows(table_t), parity))
    layer_out, pieces = layer(received, place, member, seg_ids, w_uvqk, w_out, cotangent)
    arrived = exchange(pieces)
    grad_t, squares = add_rows(asked, arrived, parity)
    squares = squares + swap_cols(squares, 1)
    squares = [squares] + [swap_cols(squares, 2 * k) for k in range(1, COLS // 2)]
    new_table_t, new_state = update(
        squares, ada_state.reshape(TOUCH // 128, 128), table_t, grad_t
    )
    return (layer_out, new_table_t.T, new_state.reshape(TOUCH))


def solution(mesh):
    in_specs = (
        P("table", "col"),
        P("table"),
        P(),
        P(),
        P("table", None, None),
        P("table", None),
        P(("table", "col"), None),
        P(("table", "col"), None),
    )
    out_specs = (P(("table", "col"), None), P("table", "col"), P("table"))
    return jax.shard_map(shards, mesh=mesh, in_specs=in_specs, out_specs=out_specs, check_vma=False)
```

```python
import functools

import jax
import jax.numpy as jnp
from jax import lax
from jax.experimental import pallas as pl
from jax.experimental.pallas import tpu as pltpu
from jax.sharding import PartitionSpec as P

D = 512
HEADS = 4
HDIM = 128
TOK_DEV = 640
TABLES = 16
COLS = 8
CAP = 80
HALF = CAP // 2
TOUCH = 2048
WIDTH = D // COLS
HI = 256
HI_BITS = 8
LO = TOUCH // HI
ASKS = 640
BLOCK = 128
REACH = 288
DEPTH = 2
PAIR = 2 * ASKS
REACH_TILES = 384
FAR = -64.0

NORM_EPS = 1e-05
ROOT_EPS = 1e-08
STEP_SIZE = 0.3

F32 = jnp.float32
BF16 = jnp.bfloat16
I32 = jnp.int32


def iota(shape, dim):
    return lax.broadcasted_iota(I32, shape, dim)


def nt_dot(a, b):
    return lax.dot_general(a, b, (((1,), (1,)), ((), ())), preferred_element_type=F32)


def tn_dot(a, b):
    return lax.dot_general(a, b, (((0,), (0,)), ((), ())), preferred_element_type=F32)


def params(megabytes):
    return pltpu.CompilerParams(vmem_limit_bytes=megabytes * 1024 * 1024)


def spans_of(row_ref):
    return [row_ref[:, TOK_DEV * m : TOK_DEV * (m + 1)] for m in range(COLS)]


def hits_of(owner_ref):
    table = iota((TABLES, TOK_DEV), 0)
    return [jnp.where(owner == table, 1.0, 0.0) for owner in spans_of(owner_ref)]


def ask_kernel(owner_ref, slot_ref, asks_ref, place_ref):
    lower = jnp.where(iota((128, 128), 0) <= iota((128, 128), 1), 1.0, 0.0).astype(BF16)
    hits = hits_of(owner_ref)
    chunks = [slice(128 * j, 128 * (j + 1)) for j in range(TOK_DEV // 128)]
    stacked = jnp.concatenate([hit[:, chunk] for chunk in chunks for hit in hits], axis=0)
    within = jnp.dot(stacked.astype(BF16), lower, preferred_element_type=F32)
    before = jnp.zeros((COLS * TABLES, 1), F32)
    running = []
    for j in range(len(chunks)):
        part = within[COLS * TABLES * j : COLS * TABLES * (j + 1)]
        running.append(part + before)
        before = before + part[:, 127:]
    running = jnp.concatenate(running, axis=1)
    lane = iota((TABLES, 128), 1)
    slot_at = iota((128, TOK_DEV), 0)
    tiles = [jnp.zeros((TABLES, 128), F32) for _ in range(ASKS // 128)]
    members = zip(hits, spans_of(owner_ref), spans_of(slot_ref))
    for m, (hit, owner, slot) in enumerate(members):
        count = running[TABLES * m : TABLES * (m + 1)] * hit
        placing = jnp.sum(count, axis=0, keepdims=True).astype(I32) - 1
        onehot = jnp.where(slot_at == placing, 1.0, 0.0).astype(BF16)
        high = (slot >> HI_BITS).astype(F32) * hit
        low = (slot & (HI - 1)).astype(F32) * hit
        found = nt_dot(jnp.concatenate([high, low], axis=0).astype(BF16), onehot)
        value = found[:TABLES] * float(HI) + found[TABLES:]
        for h in range(2):
            begin = h * (ASKS // 2) + m * HALF
            moved = pltpu.roll(value, (begin - h * HALF) % 128, 1)
            for j in range(begin // 128, (begin + HALF - 1) // 128 + 1):
                at = lane + 128 * j
                tiles[j] = jnp.where((at >= begin) & (at < begin + HALF), moved, tiles[j])
        place_ref[m : m + 1, :] = (
            owner * HALF + placing + jnp.where(placing >= HALF, TABLES * HALF - HALF, 0)
        )
    for j, tile in enumerate(tiles):
        asks_ref[:, 0, 128 * j : 128 * (j + 1)] = tile.astype(I32)


def make_asks(owner, slot):
    return pl.pallas_call(
        ask_kernel,
        out_shape=(
            jax.ShapeDtypeStruct((TABLES, 1, ASKS), I32),
            jax.ShapeDtypeStruct((COLS, TOK_DEV), I32),
        ),
        name="ask",
    )(owner, slot)


def ask_pair(asks_ref, i):
    even, odd = asks_ref[2 * i], asks_ref[2 * i + 1]
    first = iota((1, ASKS), 1) < ASKS // 2
    low = jnp.where(first, even, pltpu.roll(odd, ASKS // 2, 1))
    high = jnp.where(first, pltpu.roll(even, ASKS // 2, 1), odd)
    return jnp.concatenate([low, high], axis=1)


def ask_onehot(ask):
    rows = iota((HI, PAIR), 0).astype(F32).astype(BF16)
    wanted = (ask & (HI - 1)).astype(F32).astype(BF16)
    return jnp.where(rows == wanted, jnp.ones((), BF16), jnp.zeros((), BF16))


def rows_kernel(table_ref, rows_ref):
    for lo in range(LO):
        rows_ref[WIDTH * lo : WIDTH * (lo + 1), :] = table_ref[:, HI * lo : HI * (lo + 1)].astype(BF16)


def make_rows(table_t):
    return pl.pallas_call(
        rows_kernel,
        out_shape=jax.ShapeDtypeStruct((LO * WIDTH, HI), BF16),
        compiler_params=params(8),
        name="rows",
    )(table_t)


def pick_kernel(parity, asks_ref, rows_ref, reply_ref):
    par = parity()

    def two_groups(i, carry):
        ask = ask_pair(asks_ref, i)
        found = jnp.dot(rows_ref[...], ask_onehot(ask), preferred_element_type=F32)
        low = jnp.broadcast_to(ask >> HI_BITS, (WIDTH, PAIR))
        parts = [found[WIDTH * lo : WIDTH * (lo + 1)] for lo in range(LO)]
        for bit in (1, 2, 4):
            upper = (low & bit) != 0
            parts = [jnp.where(upper, parts[i + 1], parts[i]) for i in range(0, len(parts), 2)]
        kept = parts[0]
        first, second = kept[:, :ASKS], kept[:, ASKS:]
        stacked = jnp.concatenate(
            [jnp.where(par == 0, first, second), jnp.where(par == 0, second, first)], axis=0
        )
        replies = stacked.T.astype(BF16)
        reply_ref[2 * i] = replies[: COLS * HALF]
        reply_ref[2 * i + 1] = replies[COLS * HALF :]
        return carry

    lax.fori_loop(0, TABLES // 2, two_groups, 0, unroll=8)


def pick_rows(asks, rows, parity):
    return pl.pallas_call(
        functools.partial(pick_kernel, parity),
        out_shape=jax.ShapeDtypeStruct((TABLES, COLS * HALF, 128), BF16),
        compiler_params=params(32),
        name="pick",
    )(asks, rows)


def add_kernel(parity, asks_ref, arrived_ref, grad_ref, squares_ref, total_ref):
    par = parity()
    total_ref[...] = jnp.zeros_like(total_ref)

    def two_groups(i, carry):
        ask = ask_pair(asks_ref, i)
        block = jnp.concatenate([arrived_ref[2 * i], arrived_ref[2 * i + 1]], axis=0).astype(F32).T
        upper, lower = block[:WIDTH], block[WIDTH:]
        slots = jnp.concatenate(
            [jnp.where(par == 0, upper, lower), jnp.where(par == 0, lower, upper)], axis=1
        )
        low = jnp.broadcast_to(ask >> HI_BITS, (WIDTH, PAIR))
        spread = jnp.concatenate(
            [jnp.where(low == lo, slots, 0.0).astype(BF16) for lo in range(LO)], axis=0
        )
        total_ref[...] += nt_dot(spread, ask_onehot(ask))
        return carry

    lax.fori_loop(0, TABLES // 2, two_groups, 0, unroll=8)
    sums = []
    for lo in range(LO):
        part = total_ref[WIDTH * lo : WIDTH * (lo + 1), :]
        grad_ref[:, HI * lo : HI * (lo + 1)] = part
        square = jnp.sum(part * part, axis=0, keepdims=True)
        sums += [square[:, :128], square[:, 128:]]
    squares_ref[...] = jnp.concatenate(sums, axis=0)


def add_rows(asks, arrived, parity):
    return pl.pallas_call(
        functools.partial(add_kernel, parity),
        out_shape=(
            jax.ShapeDtypeStruct((WIDTH, TOUCH), F32),
            jax.ShapeDtypeStruct((TOUCH // 128, 128), F32),
        ),
        scratch_shapes=[pltpu.VMEM((LO * WIDTH, HI), F32)],
        compiler_params=params(48),
        name="add",
    )(asks, arrived)


def update_kernel(own_ref, near_ref, far_ref, last_ref, state_ref, table_ref, grad_ref, new_table_ref, new_state_ref):
    squares = (own_ref[...] + near_ref[...]) + (far_ref[...] + last_ref[...])
    state = state_ref[...] + squares / D
    new_state_ref[...] = state
    factor = STEP_SIZE / (jnp.sqrt(state) + ROOT_EPS)
    for i in range(TOUCH // 128):
        at = slice(128 * i, 128 * (i + 1))
        new_table_ref[:, at] = table_ref[:, at] - grad_ref[:, at] * factor[i : i + 1]


def update(squares, state, table_t, grad_t):
    return pl.pallas_call(
        update_kernel,
        out_shape=(
            jax.ShapeDtypeStruct((WIDTH, TOUCH), F32),
            jax.ShapeDtypeStruct((TOUCH // 128, 128), F32),
        ),
        compiler_params=params(16),
        name="update",
    )(*squares, state, table_t, grad_t)


def normalise(values):
    center = values - jnp.mean(values, axis=-1, keepdims=True)
    root = lax.rsqrt(jnp.mean(center * center, axis=-1, keepdims=True) + NORM_EPS)
    return center * root, root


def normalise_back(grad, normed, root):
    along = jnp.mean(grad * normed, axis=-1, keepdims=True)
    return root * (grad - jnp.mean(grad, axis=-1, keepdims=True) - normed * along)


def columns_of(row):
    return jnp.broadcast_to(row.astype(F32), (128, TOK_DEV)).T


def layer_kernel(
    member,
    received_ref,
    place_ref,
    segment_ref,
    w_ref,
    w_out_ref,
    cotangent_ref,
    out_hbm,
    pieces_ref,
    out_ref,
    left_sem,
    slots_ref,
    segment_col,
    embedded_ref,
    normed_ref,
    gates_ref,
    slope_ref,
    values_ref,
    queries_ref,
    keys_ref,
    weights_ref,
    score_slope_ref,
    attended_ref,
    grad_attended_ref,
    grad_queries_ref,
    grad_u_ref,
    token_grad_ref,
):
    place = place_ref[pl.ds(member(), 1), :]
    segment_col[...] = columns_of(segment_ref[...])
    left = iota((HALF, 128), 1) < WIDTH
    four = 4 * HALF
    units = [
        (j, h, slice(BLOCK * j, min(TOK_DEV, BLOCK * j + REACH)), slice(BLOCK * j, BLOCK * (j + 1)), slice(HDIM * h, HDIM * (h + 1)))
        for j in range(TOK_DEV // BLOCK)
        for h in range(HEADS)
    ]

    def gather_slots(t, carry):
        parts = []
        for i in range(4):
            block = received_ref[4 * t + i].astype(F32)
            parts.append([block[HALF * c : HALF * (c + 1)] for c in range(COLS)])
        at = four * t
        for j in range(COLS // 2):
            pairs = [(part[2 * j], part[2 * j + 1]) for part in parts]
            first = [jnp.where(left, even, odd) for even, odd in pairs]
            second = [pltpu.roll(jnp.where(left, odd, even), WIDTH, 1) for even, odd in pairs]
            tile = slice(128 * j, 128 * (j + 1))
            slots_ref[slice(at, at + four), tile] = jnp.concatenate(first, axis=0).astype(BF16)
            slots_ref[slice(TABLES * HALF + at, TABLES * HALF + at + four), tile] = jnp.concatenate(second, axis=0).astype(BF16)
        return carry

    for t in range(TABLES // 4):
        gather_slots(t, 0)

    at = columns_of(place).astype(I32)
    lane = iota((TOK_DEV, 128), 1)
    onehot = jnp.concatenate(
        [jnp.where(at == lane + 128 * j, 1.0, 0.0).astype(BF16) for j in range(TABLES * CAP // 128)],
        axis=1,
    )
    embedded = jnp.dot(onehot, slots_ref[...], preferred_element_type=F32)
    embedded_ref[...] = embedded.astype(BF16)
    normed, root = normalise(embedded)
    normed_ref[...] = normed.astype(BF16)
    piece = 256
    def project(p):
        return jnp.dot(
            normed_ref[...], w_ref[:, piece * p : piece * (p + 1)], preferred_element_type=F32
        )

    ahead = project(0)
    for p in range(4 * D // piece):
        part = slice(piece * p, piece * (p + 1))
        linear = 0.5 * ahead
        if p + 1 < 4 * D // piece:
            ahead = project(p + 1)
        bend = jnp.tanh(linear)
        swish = linear + linear * bend
        gate = 0.5 + 0.5 * bend
        ref = (gates_ref, values_ref, queries_ref, keys_ref)[piece * p // D]
        within = piece * p % D
        ref[:, within : within + piece] = swish.astype(ref.dtype)
        slope_ref[:, part] = gate + swish * (1.0 - gate)

    scale = HDIM**-0.5
    attended_ref[...] = jnp.zeros_like(attended_ref)
    def score(unit):
        j, h, rows, keys, head = unit
        return nt_dot(queries_ref[rows, head], keys_ref[keys, head])

    ahead = [score(units[u]) for u in range(DEPTH)]
    for u, (j, h, rows, keys, head) in enumerate(units):
        length = rows.stop - rows.start
        allowed = segment_col[rows, :] == segment_ref[:, keys].astype(F32)
        allowed = allowed & (iota((length, BLOCK), 0) >= iota((length, BLOCK), 1))
        scores = ahead.pop(0)
        if u + DEPTH < len(units):
            ahead.append(score(units[u + DEPTH]))
        scores = jnp.where(allowed, scores * (0.5 * scale), FAR)
        bend = jnp.tanh(scores)
        swish = scores + scores * bend
        gate = 0.5 + 0.5 * bend
        weights = swish.astype(BF16)
        weights_ref[HEADS * j + h, :, :length] = weights.T
        score_slope_ref[HEADS * j + h, :length, :] = scale * (gate + swish * (1.0 - gate))
        attended_ref[rows, head] += jnp.dot(weights, values_ref[keys, head], preferred_element_type=F32)

    again, root_again = normalise(attended_ref[...])
    gated = (again * gates_ref[...]).astype(BF16)
    out = jnp.dot(gated, w_out_ref[...], preferred_element_type=F32)
    out_ref[...] = (out + embedded_ref[...].astype(F32)).astype(BF16)
    leaving = pltpu.make_async_copy(out_ref, out_hbm, left_sem)
    leaving.start()
    grad_gated = nt_dot(cotangent_ref[...], w_out_ref[...]).astype(BF16).astype(F32)
    grad_u_ref[:, :D] = (grad_gated * again * slope_ref[:, :D]).astype(BF16)
    grad_attended_ref[...] = normalise_back(grad_gated * gates_ref[...], again, root_again).astype(BF16)

    grad_queries_ref[...] = jnp.zeros_like(grad_queries_ref)
    def weigh_back(unit):
        j, h, rows, keys, head = unit
        return nt_dot(grad_attended_ref[rows, head], values_ref[keys, head])

    ahead = [weigh_back(units[u]) for u in range(DEPTH)]
    for u, (j, h, rows, keys, head) in enumerate(units):
        length = rows.stop - rows.start
        grad_weights = ahead.pop(0)
        if u + DEPTH < len(units):
            ahead.append(weigh_back(units[u + DEPTH]))
        grad_scores = (grad_weights * score_slope_ref[HEADS * j + h, :length, :]).astype(BF16)
        grad_queries_ref[rows, head] += jnp.dot(grad_scores, keys_ref[keys, head], preferred_element_type=F32)
        grad_values = jnp.dot(
            weights_ref[HEADS * j + h, :, :length], grad_attended_ref[rows, head], preferred_element_type=F32
        )
        grad_keys = tn_dot(grad_scores, queries_ref[rows, head])
        for k, grad in ((1, grad_values), (3, grad_keys)):
            part = slice(k * D + head.start, k * D + head.stop)
            grad_u_ref[keys, part] = (grad * slope_ref[keys, part]).astype(BF16)
    grad_u_ref[:, 2 * D : 3 * D] = (grad_queries_ref[...] * slope_ref[:, 2 * D : 3 * D]).astype(BF16)

    grad = nt_dot(grad_u_ref[...], w_ref[...])
    grad = normalise_back(grad, normed_ref[...].astype(F32), root)
    token_grad_ref[...] = (grad + cotangent_ref[...].astype(F32)).astype(BF16)

    onehot = jnp.where(place == iota((TABLES * CAP, TOK_DEV), 0), 1.0, 0.0).astype(BF16)
    half = TABLES * HALF
    for j in range(COLS // 2):
        if j % 2 == 0:
            part = slice(128 * j, 128 * (j + 2))
            sent = jnp.dot(onehot, token_grad_ref[:, part], preferred_element_type=F32)
        tile = slice(128 * (j % 2), 128 * (j % 2 + 1))
        first, second = sent[:half, tile], pltpu.roll(sent[half:, tile], WIDTH, 1)
        wide = iota((half, 128), 1) < WIDTH
        even, odd = jnp.where(wide, first, second), jnp.where(wide, second, first)
        for t in range(TABLES):
            rows = slice(HALF * t, HALF * (t + 1))
            pieces_ref[t, 2 * HALF * j : 2 * HALF * (j + 1), :] = jnp.concatenate(
                [even[rows], odd[rows]], axis=0
            ).astype(BF16)
    leaving.wait()


def layer(received, place, member, segment, w_uvqk, w_out, cotangent):
    count = TOK_DEV // BLOCK * HEADS
    return pl.pallas_call(
        functools.partial(layer_kernel, member),
        out_shape=(
            jax.ShapeDtypeStruct((TOK_DEV, D), BF16),
            jax.ShapeDtypeStruct((TABLES, COLS * HALF, 128), BF16),
        ),
        out_specs=(pl.BlockSpec(memory_space=pl.ANY), pl.BlockSpec(memory_space=pltpu.VMEM)),
        scratch_shapes=[
            pltpu.VMEM((TOK_DEV, D), BF16),
            pltpu.SemaphoreType.DMA,
            pltpu.VMEM((TABLES * CAP, D), BF16),
            pltpu.VMEM((TOK_DEV, 128), F32),
            pltpu.VMEM((TOK_DEV, D), BF16),
            pltpu.VMEM((TOK_DEV, D), BF16),
            pltpu.VMEM((TOK_DEV, D), F32),
            pltpu.VMEM((TOK_DEV, 4 * D), F32),
            pltpu.VMEM((TOK_DEV, D), BF16),
            pltpu.VMEM((TOK_DEV, D), BF16),
            pltpu.VMEM((TOK_DEV, D), BF16),
            pltpu.VMEM((count, BLOCK, REACH_TILES), BF16),
            pltpu.VMEM((count, REACH, BLOCK), F32),
            pltpu.VMEM((TOK_DEV, D), F32),
            pltpu.VMEM((TOK_DEV, D), BF16),
            pltpu.VMEM((TOK_DEV, D), F32),
            pltpu.VMEM((TOK_DEV, 4 * D), BF16),
            pltpu.VMEM((TOK_DEV, D), BF16),
        ],
        compiler_params=params(48),
        name="layer",
    )(received, place, segment, w_uvqk, w_out, cotangent)


def exchange(blocks):
    blocks = blocks.reshape(TABLES * COLS, HALF, 128)
    blocks = lax.all_to_all(blocks, ("table", "col"), split_axis=0, concat_axis=0, tiled=True)
    return blocks.reshape(TABLES, COLS * HALF, 128)


def swap_cols(values, mask):
    return lax.ppermute(values, "col", [(c, c ^ mask) for c in range(COLS)])


def shards(table_rows, ada_state, w_uvqk, w_out, tok_owner, tok_slot, seg_ids, cotangent):
    def member():
        return lax.axis_index("col")

    def parity():
        return lax.axis_index("col") % 2

    table_t = table_rows.T
    asks, place = make_asks(tok_owner.reshape(1, COLS * TOK_DEV), tok_slot)
    asked = lax.all_to_all(asks, "table", split_axis=0, concat_axis=0, tiled=True)
    received = exchange(pick_rows(asked, make_rows(table_t), parity))
    layer_out, pieces = layer(received, place, member, seg_ids, w_uvqk, w_out, cotangent)
    arrived = exchange(pieces)
    grad_t, squares = add_rows(asked, arrived, parity)
    squares = squares + swap_cols(squares, 1)
    squares = [squares] + [swap_cols(squares, 2 * k) for k in range(1, COLS // 2)]
    new_table_t, new_state = update(
        squares, ada_state.reshape(TOUCH // 128, 128), table_t, grad_t
    )
    return (layer_out, new_table_t.T, new_state.reshape(TOUCH))


def solution(mesh):
    in_specs = (
        P("table", "col"),
        P("table"),
        P(),
        P(),
        P("table", None, None),
        P("table", None),
        P(("table", "col"), None),
        P(("table", "col"), None),
    )
    out_specs = (P(("table", "col"), None), P("table", "col"), P("table"))
    return jax.shard_map(shards, mesh=mesh, in_specs=in_specs, out_specs=out_specs, check_vma=False)
```
